32 devices in a mesh: section: 4 (over y, x), dp: 4 (over z), seq: 2 (over core).
Axes of the slice: x: 2, y: 2, z: 4, core: 2. Of those that a mesh axis runs over, the one named last changes fastest.
Arguments:
- tokens: bfloat16 [8, 1024, 1024], P('dp', 'seq'), may hold values from -6 to 6
- section_in: bfloat16 [4, 1024, 5504], P('section'), may hold values from -0.1875 to 0.1875
- section_out: bfloat16 [4, 2752, 1024], P('section')
- gains: float32 [4, 1024], P('section'), may hold values from 0.25 to 1.75
- bounds: int32 [8, 4], P('dp'), may hold values from 1 to 1023, as said below
- cotangent: bfloat16 [8, 1024, 1024], P('dp', 'seq'), may hold values from -6 to 6
Outputs:
- block_out: bfloat16 [8, 1024, 1024], P('dp', 'seq', 'section')
- grad_tokens: bfloat16 [8, 1024, 1024], P('dp', 'seq', 'section')
- grad_in: float32 [4, 1024, 5504], P('section', ('dp', 'seq'))
- grad_out: float32 [4, 2752, 1024], P('section', ('dp', 'seq'))
- grad_gains: float32 [4, 1024], P('section', ('dp', 'seq'))
The draws below stay inside these ranges and needn't reach their ends.
Inputs may be any that keep to these rules, and one draw needn't show every extreme that they name: `bounds`: each row's four start positions rise strictly; in every row one document runs from the first block of 512 positions into the last.
All inputs are finite; a program needn't handle non-finite values.
Results may differ from the reference program's by a relative error of at most 0.04.
Values may be sent and summed in bfloat16 or wider, within the bound.
No kernel may reach another device: no remote copies, remote signals or barrier semaphores. Data moves between devices by JAX's collectives and lax.ppermute only.
A program may use at most 320 MiB of HBM per device.

```python
import math
import jax
import jax.numpy as jnp
from jax import lax

D = 1024
FF = 2752
HEADS = 16
FEAT_DIM = 16
WINDOW = 64
BLOCK_LEN = 512
SEQ_LEN = 1024
ROWS = 8
N_SECTION = 4


def draw_section_out(key, part):
    key = jax.random.fold_in(key, 5)
    base_draw = jax.random.normal(key, (4, FF, D), jnp.float32)
    scales = jnp.where(jnp.arange(4) % 2 == 0, 5.0 / math.sqrt(D), 1.5 / math.sqrt(FF))
    return (base_draw * scales[:, None, None]).astype(jnp.bfloat16)


def draw_bounds(key, part):
    key = jax.random.fold_in(key, 11)
    subkeys = jax.random.split(key, 4)
    second_start = jax.random.randint(subkeys[0], (ROWS,), BLOCK_LEN // 4, BLOCK_LEN // 2)
    third_start = jax.random.randint(subkeys[1], (ROWS,), SEQ_LEN - BLOCK_LEN // 2, SEQ_LEN - BLOCK_LEN // 4)
    first_draw = jax.random.randint(subkeys[2], (ROWS,), 0, 1 << 20)
    fourth_draw = jax.random.randint(subkeys[3], (ROWS,), 0, 1 << 20)
    first_start = 1 + first_draw % (second_start - 1)
    fourth_start = third_start + 1 + fourth_draw % (SEQ_LEN - 1 - third_start)
    first_start = first_start.at[0].set(1)
    fourth_start = fourth_start.at[0].set(SEQ_LEN - 1)
    return jnp.stack([first_start, second_start, third_start, fourth_start], axis=1).astype(jnp.int32)


def shard_levels(key, shape, shards, least, largest):
    level = 1.0
    for position, shards_of in shards:
        heights = jax.random.uniform(jax.random.fold_in(jax.random.fold_in(key, 6), position), (shards_of,), jnp.float32, least / len(shards), largest / len(shards))
        level = level * jnp.repeat(jnp.exp(heights), shape[position] // shards_of).reshape((-1,) + (1,) * (len(shape) - 1 - position))
    return level


def noise(rng, dims, scale, limit, shards=(), dtype=jnp.bfloat16):
    entries = jax.random.normal(rng, dims, jnp.float32) * scale
    if len(shards) > 0:
        entries = shard_levels(rng, dims, shards, -0.22, 0.18) * entries
    return jnp.clip(entries, min=-limit, max=limit).astype(dtype)


def setup_inputs(seed: int = 0) -> dict:
    splits = jax.random.split(jax.random.key(seed), 7)
    return {
        "tokens": noise(splits[0], (ROWS, SEQ_LEN, D), 1.0, 6.0, ((0, 4), (1, 2))),
        "section_in": noise(splits[1], (N_SECTION, D, 2 * FF), D ** -0.5, 0.1875, ((0, 4),)),
        "section_out": draw_section_out(jax.random.fold_in(splits[6], 71), 0),
        "gains": jnp.clip(1.0 + 0.15 * jax.random.normal(splits[3], (N_SECTION, D), jnp.float32), 0.25, 1.75),
        "bounds": draw_bounds(jax.random.fold_in(splits[6], 71), 0),
        "cotangent": noise(splits[5], (ROWS, SEQ_LEN, D), 1.0, 6.0, ((0, 4), (1, 2))),
    }


@jax.custom_vjp
def low(v):
    return lax.optimization_barrier(v.astype(jnp.bfloat16)).astype(jnp.float32)

@jax.custom_vjp
def low_back(v):
    return v

def low_keep(v):
    return (low(v), None)

def low_pass(kept, grad):
    return (grad,)

def back_keep(v):
    return (v, None)

def back_low(kept, grad):
    return (low(grad),)
low.defvjp(low_keep, low_pass)
low_back.defvjp(back_keep, back_low)
highest = lax.Precision.HIGHEST
epsilon = 1e-06

def product(left_side, right_side):
    return jnp.dot(left_side, right_side, precision=highest, preferred_element_type=jnp.float32)

def both_ways(value):
    return low_back(low(value))

def normalize(inputs, gain_row):
    return inputs * lax.rsqrt(lax.optimization_barrier(jnp.mean(inputs * inputs, axis=-1, keepdims=True)) + epsilon) * gain_row

def doc_numbers(starts, positions):
    return lax.optimization_barrier(jnp.sum((starts[None, :] <= positions[:, None]).astype(jnp.int32), axis=1))

def linear_mix(normed, pack_in, pack_out, doc_ids):
    length, model_width = normed.shape
    qk_cols = HEADS * FEAT_DIM
    value_dim = model_width // HEADS
    queries = both_ways(product(normed, pack_in[:, :qk_cols])).reshape(length, HEADS, FEAT_DIM)
    keys_rows = both_ways(product(normed, pack_in[:, qk_cols:2 * qk_cols])).reshape(length, HEADS, FEAT_DIM)
    values = both_ways(product(normed, pack_in[:, 2 * qk_cols:2 * qk_cols + model_width])).reshape(length, HEADS, value_dim)
    scores = jnp.einsum('thf,shf->hts', queries, keys_rows, precision=highest) / math.sqrt(FEAT_DIM)
    positions = jnp.arange(length)
    allowed = (positions[None, :] <= positions[:, None]) & (doc_ids[None, :] == doc_ids[:, None])
    same_block = positions[:, None] // BLOCK_LEN == positions[None, :] // BLOCK_LEN
    inner_mask = (allowed & same_block)[None]
    outer_mask = (allowed & jnp.logical_not(same_block))[None]
    inner = low_back(jnp.where(inner_mask, scores, 0.0))
    outer = jnp.where(outer_mask, scores, 0.0)
    inner_weights = jnp.where(inner_mask, 1.0 + inner + 0.5 * inner * inner, 0.0)
    outer_weights = jnp.where(outer_mask, 1.0 + outer + 0.5 * outer * outer, 0.0)
    numer = low_back(jnp.einsum('hts,shc->thc', low(inner_weights), values, precision=highest) + jnp.einsum('hts,shc->thc', outer_weights, values, precision=highest))
    denominator = lax.optimization_barrier(jnp.sum(inner_weights + outer_weights, axis=2)).T[:, :, None]
    mixture = both_ways((numer / denominator).reshape(length, model_width))
    return product(mixture, pack_out[:model_width])

def window_mix(normed, pack_in, pack_out, doc_ids):
    length, model_width = normed.shape
    head_dim = model_width // HEADS
    queries = both_ways(product(normed, pack_in[:, :model_width])).reshape(length, HEADS, head_dim)
    keys_rows = both_ways(product(normed, pack_in[:, model_width:2 * model_width])).reshape(length, HEADS, head_dim)
    values = both_ways(product(normed, pack_in[:, 2 * model_width:3 * model_width])).reshape(length, HEADS, head_dim)
    scores = low_back(jnp.einsum('thd,shd->hts', queries, keys_rows, precision=highest) / math.sqrt(head_dim))
    positions = jnp.arange(length)
    distance = positions[:, None] - positions[None, :]
    allowed = ((distance >= 0) & (distance < WINDOW) & (doc_ids[:, None] == doc_ids[None, :]))[None]
    masked = jnp.where(allowed, scores, -1e+30)
    highest_score = lax.optimization_barrier(jnp.max(masked, axis=2, keepdims=True))
    powered = jnp.where(allowed, jnp.exp(masked - highest_score), 0.0)
    soft_weights = powered / lax.optimization_barrier(jnp.sum(powered, axis=2, keepdims=True))
    mixture = both_ways(jnp.einsum('hts,shd->thd', low(soft_weights), values, precision=highest).reshape(length, model_width))
    return product(mixture, pack_out[:model_width])

def dense_mix(normed, pack_in, pack_out):
    hidden_dim = pack_out.shape[0]
    gate_rows = low_back(product(normed, pack_in[:, :hidden_dim]))
    up_rows = low_back(product(normed, pack_in[:, hidden_dim:2 * hidden_dim]))
    hidden = low(gate_rows * jax.nn.sigmoid(gate_rows) * up_rows)
    return product(hidden, pack_out)

def forward_row(inputs, pack_in, pack_out, gain_rows, starts):
    doc_ids = doc_numbers(starts, jnp.arange(inputs.shape[0]))
    stream_one = both_ways(inputs + linear_mix(low(normalize(inputs, gain_rows[0])), pack_in[0], pack_out[0], doc_ids))
    stream_two = both_ways(stream_one + dense_mix(low(normalize(stream_one, gain_rows[1])), pack_in[1], pack_out[1]))
    stream_three = both_ways(stream_two + window_mix(low(normalize(stream_two, gain_rows[2])), pack_in[2], pack_out[2], doc_ids))
    return stream_three + dense_mix(low(normalize(stream_three, gain_rows[3])), pack_in[3], pack_out[3])

def reference(tokens, section_in, section_out, gains, bounds, cotangent):
    pack_in = section_in.astype(jnp.float32)
    pack_out = section_out.astype(jnp.float32)
    gain_rows = gains.astype(jnp.float32)

    def one_row(totals, row_data):
        inputs, cotangent_row, starts = row_data

        def apply_row(stream, weights_in, weights_out, gain_table):
            return forward_row(stream, weights_in, weights_out, gain_table, starts)
        output, pullback = jax.vjp(apply_row, inputs.astype(jnp.float32), pack_in, pack_out, gain_rows)
        grad_inputs, grad_pack_in, grad_pack_out, grad_gain = pullback(cotangent_row.astype(jnp.float32))
        totals = (totals[0] + grad_pack_in, totals[1] + grad_pack_out, totals[2] + grad_gain)
        return (totals, (output.astype(jnp.bfloat16), grad_inputs.astype(jnp.bfloat16)))
    initial = (jnp.zeros_like(pack_in), jnp.zeros_like(pack_out), jnp.zeros_like(gain_rows))
    totals, (outputs, grad_rows) = lax.scan(one_row, initial, (tokens, cotangent, bounds))
    return (outputs, grad_rows, totals[0], totals[1], totals[2])
```

```python
import functools

import jax
import jax.numpy as jnp
from jax import lax
from jax.experimental import pallas as pl
from jax.experimental.pallas import tpu as pltpu
from jax.sharding import PartitionSpec as P

HEADS = 16
FEAT_DIM = 16
WINDOW = 64
CHUNKS = 4
LAG = 1
PAIRS = HEADS // 2
epsilon = 1e-06

F32 = jnp.float32
BF16 = jnp.bfloat16


def nn(a, b):
    return jnp.dot(a, b, preferred_element_type=F32)


def nt(a, b):
    return lax.dot_general(a, b, (((1,), (1,)), ((), ())), preferred_element_type=F32)


def tn(a, b):
    return lax.dot_general(a, b, (((0,), (0,)), ((), ())), preferred_element_type=F32)


def lanes(rows, width):
    return lax.broadcasted_iota(jnp.int32, (rows, width), 1)


def call(kernel, grid, in_specs, out_specs, out_shape, scratch, flops):
    return pl.pallas_call(
        kernel,
        grid=grid,
        in_specs=in_specs,
        out_specs=out_specs,
        out_shape=out_shape,
        scratch_shapes=scratch,
        compiler_params=pltpu.CompilerParams(
            vmem_limit_bytes=40 * 1024 * 1024, dimension_semantics=("arbitrary",)
        ),
        cost_estimate=pl.CostEstimate(flops=flops, bytes_accessed=flops // 512, transcendentals=0),
    )


def whole(shape):
    return pl.BlockSpec(shape, lambda p: (0,) * len(shape))


def columns(rows, start=0, row=0):
    return pl.BlockSpec((rows, 128), lambda p: (row, start + p))


def taylor_mask(doc_t, doc_s, j, m, t_axis):
    same = doc_t == doc_s
    if j == m:
        t = lax.broadcasted_iota(jnp.int32, same.shape, t_axis)
        s = lax.broadcasted_iota(jnp.int32, same.shape, 1 - t_axis)
        same = same & (s <= t)
    return jnp.where(same, 1.0, 0.0).astype(F32)


def taylor_forward_kernel(m, size, *refs):
    docc, docr, q_ref = refs[:3]
    ks, vs = refs[3 : 4 + m], refs[4 + m : 5 + 2 * m]
    mix_ref, den_ref, mask = refs[5 + 2 * m :]
    pair = pl.program_id(0)

    @pl.when(pair == 0)
    def _():
        for j in range(m + 1):
            mask[j] = taylor_mask(
                docc[m * size : (m + 1) * size, :], docr[:, j * size : (j + 1) * size], j, m, 0
            )
        den_ref[...] = jnp.zeros_like(den_ref)

    q = q_ref[...]
    wide = lanes(size, 2 * 128) // FEAT_DIM
    lane = lanes(size, 128)
    ratios = []
    dens = den_ref[...]
    for i in range(2):
        head = 2 * pair + i
        q_head = jnp.where(wide == head, q * jnp.asarray(0.25, BF16), jnp.zeros_like(q))
        numer = jnp.zeros((size, 128), F32)
        denom = jnp.zeros((size, 1), F32)
        for j in range(m + 1):
            a = nt(q_head, ks[j][...])
            w = (1.0 + a * (1.0 + 0.5 * a)) * mask[j]
            denom += jnp.sum(w, axis=1, keepdims=True)
            numer += nn(w.astype(BF16), vs[j][...])
        ratios.append(numer / denom)
        dens = jnp.where(lane == head, denom, dens)
    den_ref[...] = dens
    mix_ref[...] = jnp.where(lane < 64, ratios[0], ratios[1]).astype(BF16)


def taylor_forward(m, docs, kept):
    size = kept[0].shape[0]
    docc, docr = docs
    return call(
        functools.partial(taylor_forward_kernel, m, size),
        (PAIRS,),
        [whole(docc.shape), whole(docr.shape), whole((size, 256))]
        + [pl.BlockSpec((size, 256), lambda p: (0, 1))] * (m + 1)
        + [columns(size, 4)] * (m + 1),
        [columns(size), whole((size, 128))],
        [
            jax.ShapeDtypeStruct((size, HEADS * 64), BF16),
            jax.ShapeDtypeStruct((size, 128), F32),
        ],
        [pltpu.VMEM((m + 1, size, size), F32)],
        2 * HEADS * (m + 1) * size * size * 512,
    )(docc, docr, kept[m], *kept, *kept)


def taylor_backward_kernel(m, size, later, *refs):
    docc, docr, q_ref = refs[:3]
    refs = refs[3:]
    ks, vs = refs[: m + 1], refs[m + 1 : 2 * m + 2]
    dmix_ref, mix_ref, den_ref = refs[2 * m + 2 : 2 * m + 5]
    refs = refs[2 * m + 5 :]
    if later:
        dk_in, dv_in = refs[:2]
        refs = refs[2:]
    dq_ref, dk_ref, dv_ref, mask, k_turned, dq_turned = refs
    pair = pl.program_id(0)

    @pl.when(pair == 0)
    def _():
        for j in range(m + 1):
            mask[j] = taylor_mask(
                docr[:, m * size : (m + 1) * size], docc[j * size : (j + 1) * size, :], j, m, 1
            )
            k_turned[j] = (ks[j][...].astype(F32) * 0.25).T.astype(BF16)
        dk_ref[...] = dk_in[...] if later else jnp.zeros_like(dk_ref)

    q = q_ref[...]
    wide = lanes(size, 2 * 128) // FEAT_DIM
    lane = lanes(size, 128)
    dm = dmix_ref[...].astype(F32)
    both = dm * mix_ref[...].astype(F32)
    den = den_ref[...]
    for i in range(2):
        head = 2 * pair + i
        inside = lane // 64 == i
        spare = 64 * (1 - i)
        turn = 1.0 / jnp.sum(jnp.where(lane == head, den, 0.0), axis=1, keepdims=True)
        dden = -jnp.sum(jnp.where(inside, both, 0.0), axis=1, keepdims=True) * turn
        dden_high = dden.astype(BF16).astype(F32)
        dnum = jnp.where(inside, dm * turn, 0.0)
        dnum_low = dnum.astype(BF16)
        dnum_more = jnp.where(
            lane == spare, dden_high, jnp.where(lane == spare + 1, dden - dden_high, dnum)
        ).astype(BF16)
        q_head = jnp.where(wide == head, q * jnp.asarray(0.25, BF16), jnp.zeros_like(q))
        own = pl.ds(pl.multiple_of(head * FEAT_DIM, FEAT_DIM), FEAT_DIM)
        dq_head = jnp.zeros((FEAT_DIM, size), F32)
        for j in range(m + 1):
            rows = pl.ds(j * size, size)
            v = vs[j][...]
            v_more = jnp.where(
                inside,
                v,
                jnp.where((lane == spare) | (lane == spare + 1), jnp.ones_like(v), jnp.zeros_like(v)),
            )
            a = nt(ks[j][...], q_head)
            w = (1.0 + a * (1.0 + 0.5 * a)) * mask[j]
            dw = nt(v_more, dnum_more)
            da = (dw * (1.0 + a) * mask[j]).astype(BF16)
            dv = nn(w.astype(BF16), dnum_low)
            if i == 0:
                dv_ref[rows, :] = dv_in[rows, :] + dv if later else dv
            else:
                dv_ref[rows, :] += dv
            dk_ref[rows, :] += nn(da, q_head)
            dq_head += nn(k_turned[j, own, :], da)
        dq_turned[own, :] = dq_head

    @pl.when(pair == PAIRS - 1)
    def _():
        dq_ref[...] = dq_turned[...].T


def taylor_backward(m, docs, kept, dmix, mix_at, den, later):
    size = kept[0].shape[0]
    docc, docr = docs
    rows = (m + 1) * size
    return call(
        functools.partial(taylor_backward_kernel, m, size, later is not None),
        (PAIRS,),
        [whole(docc.shape), whole(docr.shape), whole((size, 256))]
        + [pl.BlockSpec((size, 256), lambda p: (0, 1))] * (m + 1)
        + [columns(size, 4)] * (m + 1)
        + [columns(size), columns(size, mix_at), whole((size, 128))]
        + ([whole((rows, 256)), columns(rows)] if later is not None else []),
        [whole((size, 256)), whole((rows, 256)), columns(rows)],
        [
            jax.ShapeDtypeStruct((size, 256), F32),
            jax.ShapeDtypeStruct((rows, 256), F32),
            jax.ShapeDtypeStruct((rows, HEADS * 64), F32),
        ],
        [
            pltpu.VMEM((m + 1, size, size), F32),
            pltpu.VMEM((m + 1, 256, size), BF16),
            pltpu.VMEM((256, size), F32),
        ],
        5 * HEADS * (m + 1) * size * size * 512,
    )(docc, docr, kept[m], *kept, *kept, dmix, kept[m], den, *(later or ()))


STEP = 128


def window_spans(m, size):
    lead = STEP if m > 0 else 0
    for b in range(size // STEP):
        first = max(b * STEP + lead - STEP, 0)
        yield b * STEP, first, b * STEP + lead + STEP - first, lead


def window_mask(doc_t, doc_s, lead_rows, t_axis):
    t = lax.broadcasted_iota(jnp.int32, (doc_t == doc_s).shape, t_axis)
    s = lax.broadcasted_iota(jnp.int32, (doc_t == doc_s).shape, 1 - t_axis)
    distance = t + lead_rows - s
    return (distance >= 0) & (distance < WINDOW) & (doc_t == doc_s)


def joined(before, own):
    return jnp.concatenate([before[...], own[...]], axis=0) if before is not None else own[...]


def window_forward_kernel(m, size, *refs):
    docc, docr, q_ref, k_ref, v_ref = refs[:5]
    before_k, before_v = refs[5:7] if m > 0 else (None, None)
    mix_ref = refs[-1]
    k_all, v_all = joined(before_k, k_ref), joined(before_v, v_ref)
    lane = lanes(STEP, 128)
    for row, first, count, lead in window_spans(m, size):
        at = m * size - lead + first
        q = q_ref[row : row + STEP, :]
        k, v = k_all[first : first + count], v_all[first : first + count]
        mask = window_mask(
            docc[m * size + row : m * size + row + STEP, :],
            docr[:, at : at + count],
            row + lead - first,
            0,
        )
        mixes = []
        for i in range(2):
            q_head = jnp.where(lane // 64 == i, q * jnp.asarray(0.125, BF16), jnp.zeros_like(q))
            a = jnp.where(mask, nt(q_head, k), -1e30)
            p = jnp.exp(a - jnp.max(a, axis=1, keepdims=True))
            p = p * (1.0 / jnp.sum(p, axis=1, keepdims=True))
            mixes.append(nn(p.astype(BF16), v))
        mix_ref[row : row + STEP, :] = jnp.where(lane < 64, mixes[0], mixes[1]).astype(BF16)


def window_sources(m, size, kept, kept_before):
    last = size // STEP - 1
    specs = [columns(size), columns(size, 8), columns(size, 16)]
    arrays = [kept] * 3
    if m > 0:
        specs += [columns(STEP, 8, last), columns(STEP, 16, last)]
        arrays += [kept_before] * 2
    return specs, arrays


def window_forward(m, docs, kept, kept_before):
    size = kept.shape[0]
    docc, docr = docs
    specs, arrays = window_sources(m, size, kept, kept_before)
    return call(
        functools.partial(window_forward_kernel, m, size),
        (PAIRS,),
        [whole(docc.shape), whole(docr.shape)] + specs,
        columns(size),
        jax.ShapeDtypeStruct((size, HEADS * 64), BF16),
        [],
        2 * HEADS * size * 256 * 512,
    )(docc, docr, *arrays)


def window_backward_kernel(m, size, later, *refs):
    docc, docr, q_ref, k_ref, v_ref = refs[:5]
    refs = refs[5:]
    before_k, before_v = None, None
    if m > 0:
        before_k, before_v = refs[:2]
        refs = refs[2:]
    dmix_ref = refs[0]
    refs = refs[1:]
    if later:
        dk_in, dv_in = refs[:2]
        refs = refs[2:]
    dq_ref, dk_ref, dv_ref = refs[:3]
    refs = refs[3:]
    if m > 0:
        dk_out, dv_out = refs[:2]
        refs = refs[2:]
    dk_sum, dv_sum = refs
    lead = STEP if m > 0 else 0
    rows = size + lead
    dk_sum[...] = jnp.zeros_like(dk_sum)
    dv_sum[...] = jnp.zeros_like(dv_sum)
    if later:
        dk_sum[rows - STEP : rows, :] = dk_in[...]
        dv_sum[rows - STEP : rows, :] = dv_in[...]
    k_all, v_all = joined(before_k, k_ref), joined(before_v, v_ref)
    lane = lanes(STEP, 128)
    for row, first, count, _ in window_spans(m, size):
        at = m * size - lead + first
        q, dm = q_ref[row : row + STEP, :], dmix_ref[row : row + STEP, :]
        k, v = k_all[first : first + count], v_all[first : first + count]
        mask = window_mask(
            docr[:, m * size + row : m * size + row + STEP],
            docc[at : at + count, :],
            row + lead - first,
            1,
        )
        dq = jnp.zeros((STEP, 128), F32)
        dk = jnp.zeros((count, 128), F32)
        dv = jnp.zeros((count, 128), F32)
        for i in range(2):
            inside = lane // 64 == i
            q_head = jnp.where(inside, q * jnp.asarray(0.125, BF16), jnp.zeros_like(q))
            dm_head = jnp.where(inside, dm, jnp.zeros_like(dm))
            k_head = jnp.where(
                lanes(count, 128) // 64 == i, k * jnp.asarray(0.125, BF16), jnp.zeros_like(k)
            )
            a = jnp.where(mask, nt(k, q_head), -1e30)
            p = jnp.exp(a - jnp.max(a, axis=0, keepdims=True))
            p = p * (1.0 / jnp.sum(p, axis=0, keepdims=True))
            dp = nt(v, dm_head)
            da = (p * (dp - jnp.sum(p * dp, axis=0, keepdims=True))).astype(BF16)
            dk += nn(da, q_head)
            dv += nn(p.astype(BF16), dm_head)
            dq += tn(da, k_head)
        dq_ref[row : row + STEP, :] = dq.astype(BF16)
        dk_sum[first : first + count, :] += dk
        dv_sum[first : first + count, :] += dv
    dk_ref[...] = dk_sum[lead:rows, :].astype(BF16)
    dv_ref[...] = dv_sum[lead:rows, :].astype(BF16)
    if m > 0:
        dk_out[...] = dk_sum[:STEP, :]
        dv_out[...] = dv_sum[:STEP, :]


def window_backward(m, docs, kept, kept_before, dmix, later):
    size = kept.shape[0]
    docc, docr = docs
    specs, arrays = window_sources(m, size, kept, kept_before)
    rows = size + (STEP if m > 0 else 0)
    low = jax.ShapeDtypeStruct((size, HEADS * 64), BF16)
    edge = jax.ShapeDtypeStruct((STEP, HEADS * 64), F32)
    return call(
        functools.partial(window_backward_kernel, m, size, later is not None),
        (PAIRS,),
        [whole(docc.shape), whole(docr.shape)]
        + specs
        + [columns(size)]
        + ([columns(STEP)] * 2 if later is not None else []),
        [columns(size)] * 3 + ([columns(STEP)] * 2 if m > 0 else []),
        [low] * 3 + ([edge] * 2 if m > 0 else []),
        [pltpu.VMEM((rows, 128), F32), pltpu.VMEM((rows, 128), F32)],
        5 * HEADS * size * 256 * 512,
    )(docc, docr, *arrays, dmix, *(later or ()))


def rms_forward(inputs, gain_row):
    inverse = lax.rsqrt(jnp.mean(inputs * inputs, axis=-1, keepdims=True) + epsilon)
    return ((inputs * inverse * gain_row).astype(BF16), inverse)


def rms_backward(entry, gain_row, upstream, grad_normed):
    inputs = entry.astype(F32)
    inverse = lax.rsqrt(jnp.mean(inputs * inputs, axis=-1, keepdims=True) + epsilon)
    scaled = grad_normed * gain_row
    grad_inputs = inverse * scaled - inputs * inverse**3 * jnp.mean(
        scaled * inputs, axis=-1, keepdims=True
    )
    grad_gain = jnp.sum(grad_normed * inputs * inverse, axis=0)
    return ((upstream.astype(F32) + grad_inputs).astype(BF16), grad_gain)


def local(tokens, section_in, section_out, gains, bounds, cotangent):
    section = lax.axis_index("section")
    seq = lax.axis_index("seq")
    sections = lax.axis_size("section")
    pack_in = section_in[0]
    pack_out = section_out[0]
    gain_row = gains[0]
    _, block, width = tokens.shape
    hidden_dim = pack_out.shape[0]
    both = 2 * hidden_dim
    length = 2 * block
    size = length // CHUNKS
    last = sections - 1
    taylor_cols = 2 * HEADS * FEAT_DIM + width
    window_cols = 3 * width

    def swapped(two):
        away = lax.dynamic_index_in_dim(two, 1 - seq, 0, keepdims=False)
        own = lax.dynamic_index_in_dim(two, seq, 0, keepdims=False)
        came = lax.ppermute(away, "seq", [(0, 1), (1, 0)])
        return jnp.where(seq == 0, jnp.stack([own, came]), jnp.stack([came, own]))

    starts = lax.dynamic_index_in_dim(bounds, seq, 0, keepdims=False)
    positions = jnp.arange(length, dtype=jnp.int32)
    docs = jnp.sum((starts[None, :] <= positions[:, None]).astype(jnp.int32), axis=1)
    docs = (docs[:, None], docs[None, :])

    feed = swapped(jnp.where(section == 0, tokens, cotangent)).reshape(CHUNKS, size, width)

    turns = CHUNKS + LAG * last
    entries, kepts, denoms, finals = [], [], [], [None] * CHUNKS

    def forward_branch(s, t, entry):
        m = t - LAG * s
        if m < 0 or m >= CHUNKS:
            return lambda: (
                jnp.zeros((size, width), BF16),
                jnp.zeros((size, both), BF16),
                jnp.zeros((size, 128), F32),
            )

        def padded(parts):
            used = sum(part.shape[1] for part in parts)
            return jnp.concatenate(list(parts) + [jnp.zeros((size, both - used), BF16)], axis=1)

        def taylor():
            inputs = entry.astype(F32)
            normed, _ = rms_forward(inputs, gain_row)
            projected = nn(normed, pack_in[:, :taylor_cols]).astype(BF16)
            mix, den = taylor_forward(m, docs, kepts[t - m :] + [projected])
            output = inputs + nn(mix, pack_out[:width])
            return output.astype(BF16), padded([projected, mix]), den

        def window():
            inputs = entry.astype(F32)
            normed, _ = rms_forward(inputs, gain_row)
            projected = nn(normed, pack_in[:, :window_cols]).astype(BF16)
            mix = window_forward(m, docs, projected, kepts[t - 1] if m > 0 else None)
            output = inputs + nn(mix, pack_out[:width])
            return output.astype(BF16), padded([projected, mix]), jnp.zeros((size, 128), F32)

        def dense():
            inputs = entry.astype(F32)
            normed, _ = rms_forward(inputs, gain_row)
            gate_up = nn(normed, pack_in)
            gate, up = gate_up[:, :hidden_dim], gate_up[:, hidden_dim:]
            hidden = (gate * jax.nn.sigmoid(gate) * up).astype(BF16)
            output = inputs + nn(hidden, pack_out)
            return output.astype(BF16), gate_up.astype(BF16), jnp.zeros((size, 128), F32)

        return (taylor, dense, window, dense)[s]

    sent = []
    for t in range(turns):
        entry = feed[min(t, CHUNKS - 1)]
        if t >= LAG:
            arrived = sent[t - LAG]
            entry = jnp.where(section == 0, entry, arrived) if t < CHUNKS else arrived
        output, kept, den = lax.switch(
            section, [forward_branch(s, t, entry) for s in range(sections)]
        )
        entries.append(entry)
        kepts.append(kept)
        denoms.append(den)
        if 0 <= t - LAG * last < CHUNKS:
            finals[t - LAG * last] = output
        if t < turns - LAG:
            sent.append(lax.ppermute(output, "section", [(i, i + 1) for i in range(last)]))

    grads_low, hiddens, upstreams = [], [], []
    gain_total = jnp.zeros((width,), F32)
    returned = [None] * CHUNKS
    taylor_later = [None] * (turns + 1)
    window_later = [None] * (turns + 1)

    def backward_branch(s, t, upstream):
        f = turns - 1 - t
        m = CHUNKS - 1 - (t - LAG * (last - s))
        taylor_m = CHUNKS - 1 - (t - LAG * last)
        window_m = CHUNKS - 1 - (t - LAG * (last - 2))
        entry, kept = entries[f], kepts[f]

        def carry_zeros():
            t_rows = max(taylor_m, 0) * size if taylor_m < CHUNKS else 0
            w_rows = STEP if 0 < window_m < CHUNKS else 0
            return (
                [jnp.zeros((t_rows, 256), F32), jnp.zeros((t_rows, width), F32)] if t_rows else [],
                [jnp.zeros((w_rows, width), F32)] * 2 if w_rows else [],
            )

        if m < 0 or m >= CHUNKS:
            return lambda: (
                jnp.zeros((size, width), BF16),
                jnp.zeros((size, both), BF16),
                jnp.zeros((size, hidden_dim), BF16),
                jnp.zeros((width,), F32),
                *carry_zeros(),
            )

        def widened(parts):
            used = sum(part.shape[1] for part in parts)
            return jnp.concatenate(list(parts) + [jnp.zeros((size, both - used), BF16)], axis=1)

        def taylor():
            dmix = nt(upstream, pack_out[:width]).astype(BF16)
            dq, dk, dv = taylor_backward(
                m,
                docs,
                kepts[f - m : f + 1],
                dmix,
                taylor_cols // 128,
                denoms[f],
                taylor_later[t],
            )
            own = slice(m * size, (m + 1) * size)
            grad = [dq.astype(BF16), dk[own].astype(BF16), dv[own].astype(BF16)]
            grad_normed = nt(jnp.concatenate(grad, axis=1), pack_in[:, :taylor_cols])
            g, grad_gain = rms_backward(entry, gain_row, upstream, grad_normed)
            carry = [dk[: m * size], dv[: m * size]] if m > 0 else []
            return g, widened(grad), jnp.zeros((size, hidden_dim), BF16), grad_gain, carry, carry_zeros()[1]

        def window():
            dmix = nt(upstream, pack_out[:width]).astype(BF16)
            results = window_backward(
                m, docs, kept, kepts[f - 1] if m > 0 else None, dmix, window_later[t]
            )
            grad = list(results[:3])
            grad_normed = nt(jnp.concatenate(grad, axis=1), pack_in[:, :window_cols])
            g, grad_gain = rms_backward(entry, gain_row, upstream, grad_normed)
            return (
                g,
                widened(grad),
                jnp.zeros((size, hidden_dim), BF16),
                grad_gain,
                carry_zeros()[0],
                list(results[3:]),
            )

        def dense():
            gate = kept[:, :hidden_dim].astype(F32)
            up = kept[:, hidden_dim:].astype(F32)
            sg = jax.nn.sigmoid(gate)
            hidden = (gate * sg * up).astype(BF16)
            grad_hidden = nt(upstream, pack_out)
            grad_gate = (grad_hidden * up * sg * (1.0 + gate * (1.0 - sg))).astype(BF16)
            grad_up = (grad_hidden * gate * sg).astype(BF16)
            grad = jnp.concatenate([grad_gate, grad_up], axis=1)
            grad_normed = nt(grad, pack_in)
            g, grad_gain = rms_backward(entry, gain_row, upstream, grad_normed)
            return g, grad, hidden, grad_gain, *carry_zeros()

        return (taylor, dense, window, dense)[s]

    sent = []
    for t in range(turns):
        m_last = CHUNKS - 1 - t
        upstream = feed[max(m_last, 0)]
        if t >= LAG:
            arrived = sent[t - LAG]
            upstream = jnp.where(section == last, upstream, arrived) if m_last >= 0 else arrived
        g, grad, hidden, grad_gain, t_carry, w_carry = lax.switch(
            section, [backward_branch(s, t, upstream) for s in range(sections)]
        )
        taylor_later[t + 1] = tuple(t_carry) or None
        window_later[t + 1] = tuple(w_carry) or None
        grads_low.append(grad)
        hiddens.append(hidden)
        upstreams.append(upstream)
        gain_total = gain_total + grad_gain
        m_first = CHUNKS - 1 - (t - LAG * last)
        if 0 <= m_first < CHUNKS:
            returned[m_first] = g
        if t < turns - LAG:
            sent.append(lax.ppermute(g, "section", [(i + 1, i) for i in range(last)]))

    def weight_branch(s):
        first = LAG * (last - s)
        picks = range(first, first + CHUNKS)

        def joined_turns(parts):
            return jnp.concatenate(parts, axis=0)

        def branch():
            entry = joined_turns([entries[turns - 1 - t] for t in picks]).astype(F32)
            normed, _ = rms_forward(entry, gain_row)
            upstream = joined_turns([upstreams[t] for t in picks])
            used = (taylor_cols, both, window_cols, both)[s]
            grad = joined_turns([grads_low[t][:, :used] for t in picks])
            if s % 2 == 1:
                hidden = joined_turns([hiddens[t] for t in picks])
            else:
                hidden = joined_turns(
                    [kepts[turns - 1 - t][:, used : used + width] for t in picks]
                )
            grad_in = tn(normed, grad).astype(BF16)
            grad_out = tn(hidden, upstream).astype(BF16)
            if s % 2 == 0:
                grad_in = jnp.pad(grad_in, ((0, 0), (0, both - used)))
                grad_out = jnp.pad(grad_out, ((0, hidden_dim - width), (0, 0)))
            return grad_in, grad_out

        return branch

    grad_in, grad_out = lax.switch(section, [weight_branch(s) for s in range(sections)])
    axes = ("dp", "seq")
    grad_in = lax.psum_scatter(grad_in, axes, scatter_dimension=0, tiled=True)
    grad_out = lax.psum_scatter(grad_out, axes, scatter_dimension=0, tiled=True)
    grad_gain = lax.psum_scatter(gain_total, axes, scatter_dimension=0, tiled=True)

    def spread(parts, source):
        two = swapped(jnp.concatenate(parts, axis=0).reshape(2, block, width))
        share = width // sections
        mine = two[:, :, source * share : (source + 1) * share]
        for target in range(sections):
            if target != source:
                piece = two[:, :, target * share : (target + 1) * share]
                came = lax.ppermute(piece, "section", [(source, target)])
                mine = jnp.where(section == target, came, mine)
        return mine

    return (
        spread(finals, last),
        spread(returned, 0),
        grad_in.astype(F32)[None],
        grad_out.astype(F32)[None],
        grad_gain[None],
    )


def solution(mesh):
    placed = (
        P("dp", "seq", None),
        P("section", None, None),
        P("section", None, None),
        P("section", None),
        P("dp", None),
        P("dp", "seq", None),
    )
    return jax.shard_map(
        local,
        mesh=mesh,
        in_specs=placed,
        out_specs=(
            P("dp", "seq", "section"),
            P("dp", "seq", "section"),
            P("section", ("dp", "seq"), None),
            P("section", ("dp", "seq"), None),
            P("section", ("dp", "seq")),
        ),
        check_vma=False,
    )
```

```python
import functools

import jax
import jax.numpy as jnp
from jax import lax
from jax.experimental import pallas as pl
from jax.experimental.pallas import tpu as pltpu
from jax.sharding import PartitionSpec as P

HEADS = 16
FEAT_DIM = 16
WINDOW = 64
CHUNKS = 4
LAG = 2
TILE = 256
PAIRS = HEADS // 2
epsilon = 1e-06

F32 = jnp.float32
BF16 = jnp.bfloat16


def nn(a, b):
    return jnp.dot(a, b, preferred_element_type=F32)


def nt(a, b):
    return lax.dot_general(a, b, (((1,), (1,)), ((), ())), preferred_element_type=F32)


def tn(a, b):
    return lax.dot_general(a, b, (((0,), (0,)), ((), ())), preferred_element_type=F32)


def lanes(rows, width):
    return lax.broadcasted_iota(jnp.int32, (rows, width), 1)


def call(kernel, grid, in_specs, out_specs, out_shape, scratch, flops):
    return pl.pallas_call(
        kernel,
        grid=grid,
        in_specs=in_specs,
        out_specs=out_specs,
        out_shape=out_shape,
        scratch_shapes=scratch,
        compiler_params=pltpu.CompilerParams(
            vmem_limit_bytes=40 * 1024 * 1024, dimension_semantics=("arbitrary",)
        ),
        cost_estimate=pl.CostEstimate(flops=flops, bytes_accessed=flops // 512, transcendentals=0),
    )


def whole(shape):
    return pl.BlockSpec(shape, lambda p: (0,) * len(shape))


def columns(rows, start=0, row=0):
    return pl.BlockSpec((rows, 128), lambda p: (row, start + p))


def taylor_mask(doc_t, doc_s, j, m, t_axis):
    same = doc_t == doc_s
    if j == m:
        t = lax.broadcasted_iota(jnp.int32, same.shape, t_axis)
        s = lax.broadcasted_iota(jnp.int32, same.shape, 1 - t_axis)
        same = same & (s <= t)
    return jnp.where(same, 1.0, 0.0).astype(F32)


def taylor_forward_kernel(m, size, *refs):
    docc, docr, q_ref = refs[:3]
    ks, vs = refs[3 : 4 + m], refs[4 + m : 5 + 2 * m]
    mix_ref, den_ref, mask = refs[5 + 2 * m :]
    pair = pl.program_id(0)

    @pl.when(pair == 0)
    def _():
        for j in range(m + 1):
            mask[j] = taylor_mask(
                docc[m * size : (m + 1) * size, :], docr[:, j * size : (j + 1) * size], j, m, 0
            )
        den_ref[...] = jnp.zeros_like(den_ref)

    q = q_ref[...]
    wide = lanes(size, 2 * 128) // FEAT_DIM
    lane = lanes(size, 128)
    ratios = []
    dens = den_ref[...]
    for i in range(2):
        head = 2 * pair + i
        q_head = jnp.where(wide == head, q * jnp.asarray(0.25, BF16), jnp.zeros_like(q))
        numer = jnp.zeros((size, 128), F32)
        denom = jnp.zeros((size, 1), F32)
        for j in range(m + 1):
            a = nt(q_head, ks[j][...])
            w = (1.0 + a * (1.0 + 0.5 * a)) * mask[j]
            denom += jnp.sum(w, axis=1, keepdims=True)
            numer += nn(w.astype(BF16), vs[j][...])
        ratios.append(numer / denom)
        dens = jnp.where(lane == head, denom, dens)
    den_ref[...] = dens
    mix_ref[...] = jnp.where(lane < 64, ratios[0], ratios[1]).astype(BF16)


def taylor_forward(m, docs, kept):
    size = kept[0].shape[0]
    docc, docr = docs
    return call(
        functools.partial(taylor_forward_kernel, m, size),
        (PAIRS,),
        [whole(docc.shape), whole(docr.shape), whole((size, 256))]
        + [pl.BlockSpec((size, 256), lambda p: (0, 1))] * (m + 1)
        + [columns(size, 4)] * (m + 1),
        [columns(size), whole((size, 128))],
        [
            jax.ShapeDtypeStruct((size, HEADS * 64), BF16),
            jax.ShapeDtypeStruct((size, 128), F32),
        ],
        [pltpu.VMEM((m + 1, size, size), F32)],
        2 * HEADS * (m + 1) * size * size * 512,
    )(docc, docr, kept[m], *kept, *kept)


def taylor_backward_kernel(m, size, later, *refs):
    docc, docr, q_ref = refs[:3]
    refs = refs[3:]
    ks, vs = refs[: m + 1], refs[m + 1 : 2 * m + 2]
    dmix_ref, mix_ref, den_ref = refs[2 * m + 2 : 2 * m + 5]
    refs = refs[2 * m + 5 :]
    if later:
        dk_in, dv_in = refs[:2]
        refs = refs[2:]
    dq_ref, dk_ref, dv_ref, mask, k_turned, dq_turned = refs
    pair = pl.program_id(0)

    @pl.when(pair == 0)
    def _():
        for j in range(m + 1):
            mask[j] = taylor_mask(
                docr[:, m * size : (m + 1) * size], docc[j * size : (j + 1) * size, :], j, m, 1
            )
            k_turned[j] = (ks[j][...].astype(F32) * 0.25).T.astype(BF16)
        dk_ref[...] = jnp.zeros_like(dk_ref)
        if later:
            dk_ref[: m * size, :] = dk_in[...]

    q = q_ref[...]
    wide = lanes(size, 2 * 128) // FEAT_DIM
    lane = lanes(size, 128)
    dm = dmix_ref[...].astype(F32)
    both = dm * mix_ref[...].astype(F32)
    den = den_ref[...]
    for i in range(2):
        head = 2 * pair + i
        inside = lane // 64 == i
        spare = 64 * (1 - i)
        turn = 1.0 / jnp.sum(jnp.where(lane == head, den, 0.0), axis=1, keepdims=True)
        dden = -jnp.sum(jnp.where(inside, both, 0.0), axis=1, keepdims=True) * turn
        dden_high = dden.astype(BF16).astype(F32)
        dnum = jnp.where(inside, dm * turn, 0.0)
        dnum_low = dnum.astype(BF16)
        dnum_more = jnp.where(
            lane == spare, dden_high, jnp.where(lane == spare + 1, dden - dden_high, dnum)
        ).astype(BF16)
        q_head = jnp.where(wide == head, q * jnp.asarray(0.25, BF16), jnp.zeros_like(q))
        own = pl.ds(pl.multiple_of(head * FEAT_DIM, FEAT_DIM), FEAT_DIM)
        dq_head = jnp.zeros((FEAT_DIM, size), F32)
        for j in range(m + 1):
            rows = pl.ds(j * size, size)
            v = vs[j][...]
            v_more = jnp.where(
                inside,
                v,
                jnp.where((lane == spare) | (lane == spare + 1), jnp.ones_like(v), jnp.zeros_like(v)),
            )
            a = nt(ks[j][...], q_head)
            w = (1.0 + a * (1.0 + 0.5 * a)) * mask[j]
            dw = nt(v_more, dnum_more)
            da = (dw * (1.0 + a) * mask[j]).astype(BF16)
            dv = nn(w.astype(BF16), dnum_low)
            if i == 0:
                dv_ref[rows, :] = dv_in[rows, :] + dv if later and j < m else dv
            else:
                dv_ref[rows, :] += dv
            dk_ref[rows, :] += nn(da, q_head)
            dq_head += nn(k_turned[j, own, :], da)
        dq_turned[own, :] = dq_head

    @pl.when(pair == PAIRS - 1)
    def _():
        dq_ref[...] = dq_turned[...].T


def taylor_backward(m, docs, kept, dmix, mix, den, later):
    size = kept[0].shape[0]
    docc, docr = docs
    rows = (m + 1) * size
    return call(
        functools.partial(taylor_backward_kernel, m, size, later is not None),
        (PAIRS,),
        [whole(docc.shape), whole(docr.shape), whole((size, 256))]
        + [pl.BlockSpec((size, 256), lambda p: (0, 1))] * (m + 1)
        + [columns(size, 4)] * (m + 1)
        + [columns(size), columns(size), whole((size, 128))]
        + ([whole((m * size, 256)), columns(m * size)] if later is not None else []),
        [whole((size, 256)), whole((rows, 256)), columns(rows)],
        [
            jax.ShapeDtypeStruct((size, 256), F32),
            jax.ShapeDtypeStruct((rows, 256), F32),
            jax.ShapeDtypeStruct((rows, HEADS * 64), F32),
        ],
        [
            pltpu.VMEM((m + 1, size, size), F32),
            pltpu.VMEM((m + 1, 256, size), BF16),
            pltpu.VMEM((256, size), F32),
        ],
        5 * HEADS * (m + 1) * size * size * 512,
    )(docc, docr, kept[m], *kept, *kept, dmix, mix, den, *(later or ()))


STEP = 128


def part(pair, start):
    return pl.ds(pl.multiple_of(start + pair * 128, 128), 128)


def window_spans(m, size):
    lead = STEP if m > 0 else 0
    for b in range(size // STEP):
        first = max(b * STEP + lead - STEP, 0)
        yield b * STEP, first, b * STEP + lead + STEP - first, lead


def window_mask(doc_t, doc_s, lead_rows, t_axis):
    t = lax.broadcasted_iota(jnp.int32, (doc_t == doc_s).shape, t_axis)
    s = lax.broadcasted_iota(jnp.int32, (doc_t == doc_s).shape, 1 - t_axis)
    distance = t + lead_rows - s
    return (distance >= 0) & (distance < WINDOW) & (doc_t == doc_s)


def joined(before, own):
    return jnp.concatenate([before[...], own[...]], axis=0) if before is not None else own[...]


def window_forward_kernel(m, size, *refs):
    docc, docr, q_ref, k_ref, v_ref = refs[:5]
    before_k, before_v = refs[5:7] if m > 0 else (None, None)
    mix_ref = refs[-1]
    k_all, v_all = joined(before_k, k_ref), joined(before_v, v_ref)
    lane = lanes(STEP, 128)
    for row, first, count, lead in window_spans(m, size):
        at = m * size - lead + first
        q = q_ref[row : row + STEP, :]
        k, v = k_all[first : first + count], v_all[first : first + count]
        mask = window_mask(
            docc[m * size + row : m * size + row + STEP, :],
            docr[:, at : at + count],
            row + lead - first,
            0,
        )
        mixes = []
        for i in range(2):
            q_head = jnp.where(lane // 64 == i, q * jnp.asarray(0.125, BF16), jnp.zeros_like(q))
            a = jnp.where(mask, nt(q_head, k), -1e30)
            p = jnp.exp(a - jnp.max(a, axis=1, keepdims=True))
            p = p * (1.0 / jnp.sum(p, axis=1, keepdims=True))
            mixes.append(nn(p.astype(BF16), v))
        mix_ref[row : row + STEP, :] = jnp.where(lane < 64, mixes[0], mixes[1]).astype(BF16)


def window_sources(m, size, kept, kept_before):
    last = size // STEP - 1
    specs = [columns(size), columns(size, 8), columns(size, 16)]
    arrays = [kept] * 3
    if m > 0:
        specs += [columns(STEP, 8, last), columns(STEP, 16, last)]
        arrays += [kept_before] * 2
    return specs, arrays


def window_forward(m, docs, kept, kept_before):
    size = kept.shape[0]
    docc, docr = docs
    specs, arrays = window_sources(m, size, kept, kept_before)
    return call(
        functools.partial(window_forward_kernel, m, size),
        (PAIRS,),
        [whole(docc.shape), whole(docr.shape)] + specs,
        columns(size),
        jax.ShapeDtypeStruct((size, HEADS * 64), BF16),
        [],
        2 * HEADS * size * 256 * 512,
    )(docc, docr, *arrays)


def window_backward_kernel(m, size, later, *refs):
    docc, docr, q_ref, k_ref, v_ref = refs[:5]
    refs = refs[5:]
    before_k, before_v = None, None
    if m > 0:
        before_k, before_v = refs[:2]
        refs = refs[2:]
    dmix_ref = refs[0]
    refs = refs[1:]
    if later:
        dk_in, dv_in = refs[:2]
        refs = refs[2:]
    grad_ref = refs[0]
    refs = refs[1:]
    pair = pl.program_id(0)
    width = HEADS * 64
    if m > 0:
        dk_out, dv_out = refs[:2]
        refs = refs[2:]
    dk_sum, dv_sum = refs
    lead = STEP if m > 0 else 0
    rows = size + lead
    dk_sum[...] = jnp.zeros_like(dk_sum)
    dv_sum[...] = jnp.zeros_like(dv_sum)
    if later:
        dk_sum[rows - STEP : rows, :] = dk_in[...]
        dv_sum[rows - STEP : rows, :] = dv_in[...]
    k_all, v_all = joined(before_k, k_ref), joined(before_v, v_ref)
    lane = lanes(STEP, 128)
    for row, first, count, _ in window_spans(m, size):
        at = m * size - lead + first
        q, dm = q_ref[row : row + STEP, :], dmix_ref[row : row + STEP, :]
        k, v = k_all[first : first + count], v_all[first : first + count]
        mask = window_mask(
            docr[:, m * size + row : m * size + row + STEP],
            docc[at : at + count, :],
            row + lead - first,
            1,
        )
        dq = jnp.zeros((STEP, 128), F32)
        dk = jnp.zeros((count, 128), F32)
        dv = jnp.zeros((count, 128), F32)
        for i in range(2):
            inside = lane // 64 == i
            q_head = jnp.where(inside, q * jnp.asarray(0.125, BF16), jnp.zeros_like(q))
            dm_head = jnp.where(inside, dm, jnp.zeros_like(dm))
            k_head = jnp.where(
                lanes(count, 128) // 64 == i, k * jnp.asarray(0.125, BF16), jnp.zeros_like(k)
            )
            a = jnp.where(mask, nt(k, q_head), -1e30)
            p = jnp.exp(a - jnp.max(a, axis=0, keepdims=True))
            p = p * (1.0 / jnp.sum(p, axis=0, keepdims=True))
            dp = nt(v, dm_head)
            da = (p * (dp - jnp.sum(p * dp, axis=0, keepdims=True))).astype(BF16)
            dk += nn(da, q_head)
            dv += nn(p.astype(BF16), dm_head)
            dq += tn(da, k_head)
        grad_ref[row : row + STEP, part(pair, 0)] = dq.astype(BF16)
        dk_sum[first : first + count, :] += dk
        dv_sum[first : first + count, :] += dv
    grad_ref[:, part(pair, width)] = dk_sum[lead:rows, :].astype(BF16)
    grad_ref[:, part(pair, 2 * width)] = dv_sum[lead:rows, :].astype(BF16)
    if m > 0:
        dk_out[...] = dk_sum[:STEP, :]
        dv_out[...] = dv_sum[:STEP, :]


def window_backward(m, docs, kept, kept_before, dmix, later):
    size = kept.shape[0]
    docc, docr = docs
    specs, arrays = window_sources(m, size, kept, kept_before)
    rows = size + (STEP if m > 0 else 0)
    low = jax.ShapeDtypeStruct((size, 3 * HEADS * 64), BF16)
    edge = jax.ShapeDtypeStruct((STEP, HEADS * 64), F32)
    return call(
        functools.partial(window_backward_kernel, m, size, later is not None),
        (PAIRS,),
        [whole(docc.shape), whole(docr.shape)]
        + specs
        + [columns(size)]
        + ([columns(STEP)] * 2 if later is not None else []),
        [whole((size, 3 * HEADS * 64))] + ([columns(STEP)] * 2 if m > 0 else []),
        [low] + ([edge] * 2 if m > 0 else []),
        [pltpu.VMEM((rows, 128), F32), pltpu.VMEM((rows, 128), F32)],
        5 * HEADS * size * 256 * 512,
    )(docc, docr, *arrays, dmix, *(later or ()))


def blank(shapes):
    return pl.pallas_call(
        lambda *refs: None,
        out_specs=[pl.BlockSpec(memory_space=pl.ANY)] * len(shapes),
        out_shape=[jax.ShapeDtypeStruct(*shape) for shape in shapes],
    )()


def rms_inverse(inputs):
    return lax.rsqrt(jnp.mean(inputs * inputs, axis=-1, keepdims=True) + epsilon)


def rms_forward(inputs, gain_row):
    return (inputs * rms_inverse(inputs) * gain_row).astype(BF16)


def rms_backward(inputs, gain_row, grad_normed):
    inverse = rms_inverse(inputs)
    scaled = grad_normed * gain_row
    grad_inputs = inverse * scaled - inputs * inverse**3 * jnp.mean(
        scaled * inputs, axis=-1, keepdims=True
    )
    grad_gain = jnp.sum(grad_normed * inputs * inverse, axis=0, keepdims=True)
    return grad_inputs, grad_gain


def spans(width):
    part = width // 2 if width % 256 == 0 else width
    return [(start, part) for start in range(0, width, part)]


def begin(sems, copies):
    made = [pltpu.make_async_copy(a, b, sems.at[i]) for i, (a, b) in enumerate(copies)]
    for copy in made:
        copy.start()
    return made


def finish(copies):
    for copy in copies:
        copy.wait()


def dense_forward_kernel(
    x_ref, gain_ref, wg_ref, wu_ref, wo_ref, out_ref, gate_ref, up_ref, wg, wu, wo, gates, ups, sems, done
):
    tiles = spans(gates.shape[1])
    reads = []
    for n, (at, w) in enumerate(tiles):
        cut = pl.ds(at, w)
        reads.append(
            begin(
                sems.at[n],
                [
                    (wg_ref.at[:, cut], wg.at[:, cut]),
                    (wu_ref.at[:, cut], wu.at[:, cut]),
                    (wo_ref.at[cut, :], wo.at[cut, :]),
                ],
            )
        )
    inputs = x_ref[...].astype(F32)
    normed = rms_forward(inputs, gain_ref[...])
    total = inputs
    writes = []
    for n, (at, w) in enumerate(tiles):
        cut = pl.ds(at, w)
        reads[n][0].wait()
        gate = nn(normed, wg[:, cut])
        reads[n][1].wait()
        up = nn(normed, wu[:, cut])
        gates[:, cut] = gate.astype(BF16)
        ups[:, cut] = up.astype(BF16)
        writes += begin(
            done.at[n], [(gates.at[:, cut], gate_ref.at[:, cut]), (ups.at[:, cut], up_ref.at[:, cut])]
        )
        hidden = (gate * jax.nn.sigmoid(gate) * up).astype(BF16)
        reads[n][2].wait()
        total = total + nn(hidden, wo[cut, :])
    out_ref[...] = total.astype(BF16)
    finish(writes)


IN_VMEM = pl.BlockSpec(memory_space=pltpu.VMEM)
IN_PLACE = pl.BlockSpec(memory_space=pl.ANY)


def plain_call(kernel, in_specs, out_specs, out_shape, scratch, flops):
    return pl.pallas_call(
        kernel,
        in_specs=in_specs,
        out_specs=out_specs,
        out_shape=out_shape,
        scratch_shapes=scratch,
        compiler_params=pltpu.CompilerParams(vmem_limit_bytes=48 * 1024 * 1024),
        cost_estimate=pl.CostEstimate(flops=flops, bytes_accessed=flops // 512, transcendentals=0),
    )


def weight_scratch(width, padded):
    return [pltpu.VMEM((width, padded), BF16)] * 2 + [pltpu.VMEM((padded, width), BF16)]


def dense_forward(x, gain, weights):
    size, width = x.shape
    padded = weights[0].shape[1]
    tiles = len(spans(padded))
    return plain_call(
        dense_forward_kernel,
        [IN_VMEM, IN_VMEM] + [IN_PLACE] * 3,
        [IN_VMEM, IN_PLACE, IN_PLACE],
        [jax.ShapeDtypeStruct((size, width), BF16)]
        + [jax.ShapeDtypeStruct((size, padded), BF16)] * 2,
        weight_scratch(width, padded)
        + [pltpu.VMEM((size, padded), BF16)] * 2
        + [pltpu.SemaphoreType.DMA((tiles, 3)), pltpu.SemaphoreType.DMA((tiles, 2))],
        6 * size * width * padded,
    )(x, gain, *weights)


def dense_backward_kernel(
    x_ref,
    gain_ref,
    g_ref,
    gate_ref,
    up_ref,
    wg_ref,
    wu_ref,
    wo_ref,
    out_ref,
    dgate_ref,
    dup_ref,
    hidden_ref,
    dgain_ref,
    wg,
    wu,
    wo,
    gates,
    ups,
    dgates,
    dups,
    hiddens,
    sems,
    done,
):
    tiles = spans(gates.shape[1])
    reads = []
    for n, (at, w) in enumerate(tiles):
        cut = pl.ds(at, w)
        reads.append(
            begin(
                sems.at[n],
                [
                    (wo_ref.at[cut, :], wo.at[cut, :]),
                    (gate_ref.at[:, cut], gates.at[:, cut]),
                    (up_ref.at[:, cut], ups.at[:, cut]),
                    (wg_ref.at[:, cut], wg.at[:, cut]),
                    (wu_ref.at[:, cut], wu.at[:, cut]),
                ],
            )
        )
    g = g_ref[...]
    total = jnp.zeros(g.shape, F32)
    writes = []
    for n, (at, w) in enumerate(tiles):
        cut = pl.ds(at, w)
        finish(reads[n][:3])
        dh = nt(g, wo[cut, :])
        gate = gates[:, cut].astype(F32)
        up = ups[:, cut].astype(F32)
        sg = jax.nn.sigmoid(gate)
        active = gate * sg
        hiddens[:, cut] = (active * up).astype(BF16)
        dgate = (dh * up * (sg + active * (1.0 - sg))).astype(BF16)
        dup = (dh * active).astype(BF16)
        dgates[:, cut] = dgate
        dups[:, cut] = dup
        writes += begin(
            done.at[n],
            [
                (hiddens.at[:, cut], hidden_ref.at[:, cut]),
                (dgates.at[:, cut], dgate_ref.at[:, cut]),
                (dups.at[:, cut], dup_ref.at[:, cut]),
            ],
        )
        finish(reads[n][3:])
        total = total + nt(dgate, wg[:, cut]) + nt(dup, wu[:, cut])
    grad, dgain = rms_backward(x_ref[...].astype(F32), gain_ref[...], total)
    out_ref[...] = (g.astype(F32) + grad).astype(BF16)
    dgain_ref[...] = dgain
    finish(writes)


def dense_backward(x, gain, g, gate, up, weights):
    size, width = x.shape
    padded = weights[0].shape[1]
    tiles = len(spans(padded))
    return plain_call(
        dense_backward_kernel,
        [IN_VMEM] * 3 + [IN_PLACE] * 5,
        [IN_VMEM] + [IN_PLACE] * 3 + [IN_VMEM],
        [jax.ShapeDtypeStruct((size, width), BF16)]
        + [jax.ShapeDtypeStruct((size, padded), BF16)] * 3
        + [jax.ShapeDtypeStruct((1, width), F32)],
        weight_scratch(width, padded)
        + [pltpu.VMEM((size, padded), BF16)] * 5
        + [pltpu.SemaphoreType.DMA((tiles, 5)), pltpu.SemaphoreType.DMA((tiles, 3))],
        6 * size * width * padded,
    )(x, gain, g, gate, up, *weights)


def dense_both_kernel(
    x_ref,
    gain_ref,
    g_ref,
    wg_ref,
    wu_ref,
    wo_ref,
    final_ref,
    out_ref,
    dgate_ref,
    dup_ref,
    hidden_ref,
    dgain_ref,
    wg,
    wu,
    wo,
    dgates,
    dups,
    hiddens,
    sems,
    done,
):
    tiles = spans(dgates.shape[1])
    reads = []
    for n, (at, w) in enumerate(tiles):
        cut = pl.ds(at, w)
        reads.append(
            begin(
                sems.at[n],
                [
                    (wg_ref.at[:, cut], wg.at[:, cut]),
                    (wu_ref.at[:, cut], wu.at[:, cut]),
                    (wo_ref.at[cut, :], wo.at[cut, :]),
                ],
            )
        )
    inputs = x_ref[...].astype(F32)
    normed = rms_forward(inputs, gain_ref[...])
    g = g_ref[...]
    final = inputs
    total = jnp.zeros(g.shape, F32)
    writes = []
    for n, (at, w) in enumerate(tiles):
        cut = pl.ds(at, w)
        reads[n][0].wait()
        gate = nn(normed, wg[:, cut])
        reads[n][1].wait()
        up = nn(normed, wu[:, cut])
        sg = jax.nn.sigmoid(gate)
        active = gate * sg
        hidden = (active * up).astype(BF16)
        hiddens[:, cut] = hidden
        reads[n][2].wait()
        final = final + nn(hidden, wo[cut, :])
        dh = nt(g, wo[cut, :])
        dgate = (dh * up * (sg + active * (1.0 - sg))).astype(BF16)
        dup = (dh * active).astype(BF16)
        dgates[:, cut] = dgate
        dups[:, cut] = dup
        writes += begin(
            done.at[n],
            [
                (hiddens.at[:, cut], hidden_ref.at[:, cut]),
                (dgates.at[:, cut], dgate_ref.at[:, cut]),
                (dups.at[:, cut], dup_ref.at[:, cut]),
            ],
        )
        total = total + nt(dgate, wg[:, cut]) + nt(dup, wu[:, cut])
    final_ref[...] = final.astype(BF16)
    grad, dgain = rms_backward(inputs, gain_ref[...], total)
    out_ref[...] = (g.astype(F32) + grad).astype(BF16)
    dgain_ref[...] = dgain
    finish(writes)


def dense_both(x, gain, g, weights):
    size, width = x.shape
    padded = weights[0].shape[1]
    tiles = len(spans(padded))
    return plain_call(
        dense_both_kernel,
        [IN_VMEM] * 3 + [IN_PLACE] * 3,
        [IN_VMEM] * 2 + [IN_PLACE] * 3 + [IN_VMEM],
        [jax.ShapeDtypeStruct((size, width), BF16)] * 2
        + [jax.ShapeDtypeStruct((size, padded), BF16)] * 3
        + [jax.ShapeDtypeStruct((1, width), F32)],
        weight_scratch(width, padded)
        + [pltpu.VMEM((size, padded), BF16)] * 3
        + [pltpu.SemaphoreType.DMA((tiles, 3)), pltpu.SemaphoreType.DMA((tiles, 3))],
        12 * size * width * padded,
    )(x, gain, g, *weights)


def grad_in_kernel(count, tiles, gain_ref, *refs):
    xs, refs = refs[:count], refs[count:]
    groups = [refs[count * n : count * (n + 1)] for n in range(len(tiles))]
    out_ref, turned = refs[count * len(tiles) :]
    step = pl.program_id(0)
    size = xs[0].shape[0]

    @pl.when(step == 0)
    def _():
        for c in range(count):
            normed = rms_forward(xs[c][...].astype(F32), gain_ref[...])
            turned[:, c * size : (c + 1) * size] = normed.astype(F32).T.astype(BF16)

    start = 0
    for parts, (_, used) in zip(groups, tiles):

        @pl.when((step >= start) & (step < start + used))
        def _(parts=parts):
            joined = jnp.concatenate([part[...] for part in parts], axis=0)
            out_ref[...] = nn(turned[...], joined).astype(BF16)

        start += used


def grad_in(gain, xs, groups, out_width):
    count = len(xs)
    size, width = xs[0].shape
    specs = [whole((1, width))] + [whole((size, width))] * count
    arrays, begun = [], 0
    for parts, first, used in groups:

        def at(j, first=first, used=used, begun=begun):
            return (0, first + jnp.clip(j - begun, 0, used - 1))

        specs += [pl.BlockSpec((size, TILE), at)] * count
        arrays += parts
        begun += used
    return call(
        functools.partial(grad_in_kernel, count, [group[1:] for group in groups]),
        (begun,),
        specs,
        pl.BlockSpec((width, TILE), lambda j: (0, j)),
        jax.ShapeDtypeStruct((width, out_width), BF16),
        [pltpu.VMEM((width, count * size), BF16)],
        2 * count * size * width * TILE * begun,
    )(gain, *xs, *arrays)


def grad_out_kernel(count, used, *refs):
    left, right = refs[:count], refs[count : 2 * count]
    out_ref = refs[2 * count]
    step = pl.program_id(0)

    @pl.when(step < used)
    def _():
        joined = jnp.concatenate([part[...] for part in left], axis=0)
        turned = joined.astype(F32).T.astype(BF16)
        out_ref[...] = nn(turned, jnp.concatenate([part[...] for part in right], axis=0)).astype(
            BF16
        )

    @pl.when(step >= used)
    def _():
        out_ref[...] = jnp.zeros_like(out_ref)


def grad_out(left, right, used, rows):
    count = len(left)
    size, width = right[0].shape
    tiles = -(-rows // TILE)
    return call(
        functools.partial(grad_out_kernel, count, used),
        (tiles,),
        [pl.BlockSpec((size, TILE), lambda j: (0, jnp.minimum(j, used - 1)))] * count
        + [whole((size, width))] * count,
        pl.BlockSpec((TILE, width), lambda j: (j, 0)),
        jax.ShapeDtypeStruct((rows, width), BF16),
        [],
        2 * count * size * width * TILE * used,
    )(*left, *right)


def local(tokens, section_in, section_out, gains, bounds, cotangent):
    section = lax.axis_index("section")
    seq = lax.axis_index("seq")
    sections = lax.axis_size("section")
    pack_in = section_in[0]
    pack_out = section_out[0]
    gain_row = gains
    _, block, width = tokens.shape
    hidden_dim = pack_out.shape[0]
    padded = -(-hidden_dim // TILE) * TILE
    length = 2 * block
    size = length // CHUNKS
    taylor_cols = 2 * HEADS * FEAT_DIM + width
    window_cols = 3 * width
    last = sections - 1

    def swapped(two):
        away = lax.dynamic_index_in_dim(two, 1 - seq, 0, keepdims=False)
        own = lax.dynamic_index_in_dim(two, seq, 0, keepdims=False)
        came = lax.ppermute(away, "seq", [(0, 1), (1, 0)])
        return jnp.where(seq == 0, jnp.stack([own, came]), jnp.stack([came, own]))

    def branches(shapes, makers):
        names = list(shapes)

        def branch(maker):
            def run():
                made = maker() if maker is not None else {}
                missing = [name for name in names if name not in made]
                empty = dict(zip(missing, blank([shapes[name] for name in missing]))) if missing else {}
                return tuple(made[name] if name in made else empty[name] for name in names)

            return run

        values = lax.switch(section, [branch(maker) for maker in makers])
        return dict(zip(names, values))

    starts = lax.dynamic_index_in_dim(bounds, seq, 0, keepdims=False)
    positions = jnp.arange(length, dtype=jnp.int32)
    docs = jnp.sum((starts[None, :] <= positions[:, None]).astype(jnp.int32), axis=1)
    docs = (docs[:, None], docs[None, :])

    feed = swapped(jnp.where(section == 0, tokens, cotangent)).reshape(length, width)

    def fed(m):
        return feed[m * size : (m + 1) * size]

    first_back = (last + 1) * LAG
    pair_turn = first_back + CHUNKS - 1
    turns = pair_turn + LAG + 1
    low = ((size, width), BF16)
    wide = ((size, padded), BF16)
    edge = ((STEP, width), F32)
    gain_shape = ((1, width), F32)
    made, sent = [], []
    back_one, back_two = {}, {}

    def prepare():
        more = padded - hidden_dim
        return {
            "wg": jnp.pad(pack_in[:, :hidden_dim], ((0, 0), (0, more))),
            "wu": jnp.pad(pack_in[:, hidden_dim:], ((0, 0), (0, more))),
            "wo": jnp.pad(pack_out, ((0, more), (0, 0))),
        }

    def entry(s, m):
        return fed(m) if s == 0 else sent[m + LAG * (s - 1)]["out"]

    def upstream(s, m):
        if s == last:
            return fed(m)
        if s == 2:
            return sent[m + LAG * last]["out"]
        turn = first_back + 1 + LAG * (1 - s) + m
        if m < CHUNKS - 1:
            return sent[turn]["out"]
        return sent[turn - 1]["out2"]

    def taylor_turn(m):
        def run():
            inputs = entry(0, m).astype(F32)
            projected = nn(rms_forward(inputs, gain_row), pack_in[:, :taylor_cols]).astype(BF16)
            mix, den = taylor_forward(m, docs, [made[i]["linear"] for i in range(m)] + [projected])
            output = (inputs + nn(mix, pack_out[:width])).astype(BF16)
            return {"out": output, "linear": projected, "mix": mix, "den": den}

        return run

    def dense_turn(m):
        def run():
            out, gate, up = dense_forward(entry(1, m), gain_row, weights)
            return {"out": out, "gate": gate, "up": up}

        return run

    def window_turn(m):
        def run():
            inputs = entry(2, m).astype(F32)
            projected = nn(rms_forward(inputs, gain_row), pack_in[:, :window_cols]).astype(BF16)
            before = made[2 * LAG + m - 1]["window"] if m > 0 else None
            mix = window_forward(m, docs, projected, before)
            output = (inputs + nn(mix, pack_out[:width])).astype(BF16)
            return {"out": output, "window": projected, "mix": mix}

        return run

    def dense_both_turn(m):
        def run():
            final, out, dgate, dup, hidden, gain = dense_both(
                entry(3, m), gain_row, upstream(3, m), weights
            )
            return {
                "final": final,
                "out": out,
                "dgate": dgate,
                "dup": dup,
                "hidden": hidden,
                "gain": gain,
            }

        return run

    def window_back(m):
        def settled(m, grad, edges):
            if edges is not None:
                more = jnp.concatenate(edges, axis=1)
                tail = grad[size - STEP :, width:].astype(F32) + more
                grad = lax.dynamic_update_slice(grad, tail.astype(BF16), (size - STEP, width))
            grad_inputs, gain = rms_backward(
                entry(2, m).astype(F32), gain_row, nt(grad, pack_in[:, :window_cols])
            )
            return (upstream(2, m).astype(F32) + grad_inputs).astype(BF16), grad, gain

        def run():
            kept = made[2 * LAG + m]["window"]
            before = made[2 * LAG + m - 1]["window"] if m > 0 else None
            dmix = nt(upstream(2, m), pack_out[:width]).astype(BF16)
            results = window_backward(m, docs, kept, before, dmix, None)
            if m == 0:
                return {"part": results[0]}
            out, done, gain = settled(m - 1, made[first_back + m - 1]["part"], results[1:])
            values = {"out": out, "done": done, "gain": gain}
            if m < CHUNKS - 1:
                values["part"] = results[0]
            else:
                out, done, more = settled(m, results[0], None)
                values.update(out2=out, done2=done, gain=gain + more)
            return values

        return run

    def dense_back(ms):
        def run():
            values, gains_sum = {}, 0.0
            for n, m in enumerate(ms):
                kept = made[LAG + m]
                out, dgate, dup, hidden, gain = dense_backward(
                    entry(1, m), gain_row, upstream(1, m), kept["gate"], kept["up"], weights
                )
                more = "2" if n else ""
                values.update(
                    {"out" + more: out, "dgate" + more: dgate, "dup" + more: dup,
                     "hidden" + more: hidden}
                )
                gains_sum = gains_sum + gain
            values["gain"] = gains_sum
            return values

        return run

    def taylor_back(ms, earlier):
        dqs = []
        for m in ms:
            dmix = nt(upstream(0, m), pack_out[:width]).astype(BF16)
            dq, dk, dv = taylor_backward(
                m,
                docs,
                [made[i]["linear"] for i in range(m + 1)],
                dmix,
                made[m]["mix"],
                made[m]["den"],
                earlier,
            )
            earlier = (dk, dv)
            dqs.append(dq)
        return dqs, earlier

    def taylor_turn_back(m):
        def run():
            earlier = (made[-1]["dk"], made[-1]["dv"]) if m > 0 else None
            dqs, (dk, dv) = taylor_back([m], earlier)
            return {"dq": dqs[0], "dk": dk, "dv": dv}

        return run

    def spread(two, source):
        share = width // sections
        mine = two[:, :, source * share : (source + 1) * share]
        for target in range(sections):
            if target != source:
                piece = two[:, :, target * share : (target + 1) * share]
                came = lax.ppermute(piece, "section", [(source, target)])
                mine = jnp.where(section == target, came, mine)
        return mine

    taylor_shapes = {}
    for t in range(turns + 1):
        shapes, makers, pairs, pairs_two = {}, [None] * sections, [], []
        for s in range(sections):
            m = t - LAG * s
            if 0 <= m < CHUNKS:
                shapes["out"] = low
                makers[s] = (taylor_turn, dense_turn, window_turn, dense_both_turn)[s](m)
                if s == 0:
                    shapes.update(linear=((size, taylor_cols), BF16), mix=low)
                    shapes["den"] = ((size, 128), F32)
                elif s == 1:
                    shapes.update(gate=wide, up=wide)
                elif s == 2:
                    shapes.update(window=((size, window_cols), BF16), mix=low)
                else:
                    shapes.update(final=low, dgate=wide, dup=wide, hidden=wide, gain=gain_shape)
                pairs.append((s, s + 1) if s < last else (s, s - 1))
        if t == 0:
            shapes.update(
                wg=((width, padded), BF16), wu=((width, padded), BF16), wo=((padded, width), BF16)
            )
            makers[1] = makers[3] = prepare
        m = t - first_back
        if 0 <= m < CHUNKS:
            makers[2] = window_back(m)
            if m < CHUNKS - 1:
                shapes["part"] = ((size, window_cols), BF16)
            if m > 0:
                shapes.update(out=low, done=((size, window_cols), BF16), gain=gain_shape)
                pairs.append((2, 1))
            if m == CHUNKS - 1:
                shapes.update(out2=low, done2=((size, window_cols), BF16))
                pairs_two.append((2, 1))
        m = t - first_back - 1 - LAG
        if 0 <= m < CHUNKS - 1:
            ms = [m] if m < CHUNKS - 2 else [m, m + 1]
            makers[1] = dense_back(ms)
            shapes.update(out=low, dgate=wide, dup=wide, hidden=wide, gain=gain_shape)
            pairs.append((1, 0))
            if len(ms) > 1:
                shapes.update(out2=low, dgate2=wide, dup2=wide, hidden2=wide)
                pairs_two.append((1, 0))
        m = t - first_back - 1 - 2 * LAG
        if 0 <= m < CHUNKS - 2:
            makers[0] = taylor_turn_back(m)
            rows = (m + 1) * size
            taylor_shapes = {
                "dq": ((size, 256), F32),
                "dk": ((rows, 256), F32),
                "dv": ((rows, width), F32),
            }
            shapes.update(taylor_shapes)
        if t == turns:
            break
        made.append(branches(shapes, makers))
        if t == 0:
            weights = (made[0]["wg"], made[0]["wu"], made[0]["wo"])
        sent.append(
            {
                name: lax.ppermute(made[t][name], "section", which)
                for name, which in (("out", pairs), ("out2", pairs_two))
                if which
            }
        )

    def turns_of(s):
        if s == last:
            return [made[LAG * last + m] for m in range(CHUNKS)]
        if s == 2:
            return [made[first_back + 1 + m] for m in range(CHUNKS - 1)]
        return [made[first_back + 1 + LAG + m] for m in range(CHUNKS - 1)]

    def every(s, name):
        values = turns_of(s)
        found = [value[name] for value in values]
        return found + [values[-1][name + "2"]] if s != last else found

    def gains_of(s):
        return sum(value["gain"] for value in turns_of(s))

    def entries(s):
        return [entry(s, m) for m in range(CHUNKS)]

    def upstreams(s):
        return [upstream(s, m) for m in range(CHUNKS)]

    b_cols = taylor_cols
    a_cols = 2 * padded - b_cols
    half_tiles = padded // TILE
    a_shape, b_shape = ((width, a_cols), BF16), ((width, b_cols), BF16)

    def dense_first(s):
        def run():
            groups = [
                (every(s, "dgate"), 0, half_tiles),
                (every(s, "dup"), 0, a_cols // TILE - half_tiles),
            ]
            return {"a": grad_in(gain_row, entries(s), groups, a_cols)}

        return run

    def window_first():
        groups = [(every(2, "done"), 0, window_cols // TILE)]
        return {"a": grad_in(gain_row, entries(2), groups, a_cols)}

    def dense_second(s):
        def run():
            groups = [(every(s, "dup"), a_cols // TILE - half_tiles, b_cols // TILE)]
            return {
                "b": grad_in(gain_row, entries(s), groups, b_cols),
                "c": grad_out(every(s, "hidden"), upstreams(s), half_tiles, hidden_dim),
                "gain": gains_of(s),
            }

        return run

    def window_second():
        mixes = [made[2 * LAG + m]["mix"] for m in range(CHUNKS)]
        return {
            "c": grad_out(mixes, upstreams(2), width // TILE, hidden_dim),
            "gain": gains_of(2),
        }

    def taylor_last():
        done = CHUNKS - 2
        dqs, (dk, dv) = taylor_back(
            range(done, CHUNKS), (made[turns]["dk"], made[turns]["dv"])
        )
        dqs = [made[turns - done + 1 + m]["dq"] for m in range(done)] + dqs
        grad = jnp.concatenate([jnp.concatenate(dqs, axis=0), dk, dv], axis=1).astype(BF16)
        came = jnp.concatenate(upstreams(0), axis=0)
        grad_inputs, gain = rms_backward(
            feed.astype(F32), gain_row, nt(grad, pack_in[:, :taylor_cols])
        )
        return {
            "returned": (came.astype(F32) + grad_inputs).astype(BF16),
            "b": grad_in(gain_row, [feed], [([grad], 0, taylor_cols // TILE)], b_cols),
            "c": grad_out(
                [made[m]["mix"] for m in range(CHUNKS)], upstreams(0), width // TILE, hidden_dim
            ),
            "gain": gain,
        }

    made.append(
        branches(
            {"a": a_shape, **taylor_shapes},
            [taylor_turn_back(CHUNKS - 3), dense_first(1), window_first, dense_first(3)],
        )
    )
    axes = ("dp", "seq")
    a = made[turns]["a"]
    sum_a = lax.psum_scatter(a, axes, scatter_dimension=0, tiled=True)
    rest = branches(
        {
            "b": b_shape,
            "c": ((hidden_dim, width), BF16),
            "gain": gain_shape,
            "returned": ((length, width), BF16),
        },
        [taylor_last, dense_second(1), window_second, dense_second(3)],
    )
    sum_b = lax.psum_scatter(rest["b"], axes, scatter_dimension=0, tiled=True)
    sum_c = lax.psum_scatter(rest["c"], axes, scatter_dimension=0, tiled=True)
    out_gain = lax.psum_scatter(rest["gain"][0], axes, scatter_dimension=0, tiled=True)

    finals = [made[LAG * last + m]["final"] for m in range(CHUNKS)]
    block_out = spread(swapped(jnp.concatenate(finals, axis=0).reshape(2, block, width)), last)
    grad_tokens = spread(swapped(rest["returned"].reshape(2, block, width)), 0)

    def narrow(value, used):
        return lambda: jnp.pad(value[:, :used].astype(F32), ((0, 0), (0, 2 * hidden_dim - used)))

    def dense_result():
        up_end = padded + hidden_dim - a_cols
        return jnp.concatenate(
            [sum_a[:, :hidden_dim], sum_a[:, padded:], sum_b[:, :up_end]], axis=1
        ).astype(F32)

    out_in = lax.switch(
        section,
        [narrow(sum_b, taylor_cols), dense_result, narrow(sum_a, window_cols), dense_result],
    )
    return (
        block_out,
        grad_tokens,
        out_in[None],
        sum_c.astype(F32)[None],
        out_gain[None],
    )


def solution(mesh):
    placed = (
        P("dp", "seq", None),
        P("section", None, None),
        P("section", None, None),
        P("section", None),
        P("dp", None),
        P("dp", "seq", None),
    )
    return jax.shard_map(
        local,
        mesh=mesh,
        in_specs=placed,
        out_specs=(
            P("dp", "seq", "section"),
            P("dp", "seq", "section"),
            P("section", ("dp", "seq"), None),
            P("section", ("dp", "seq"), None),
            P("section", ("dp", "seq")),
        ),
        check_vma=False,
    )
```

```python
import functools

import jax
import jax.numpy as jnp
from jax import lax
from jax.experimental import pallas as pl
from jax.experimental.pallas import tpu as pltpu
from jax.sharding import PartitionSpec as P

HEADS = 16
FEAT_DIM = 16
WINDOW = 64
CHUNKS = 4
LAG = 2
TILE = 256
PAIRS = HEADS // 2
epsilon = 1e-06

F32 = jnp.float32
BF16 = jnp.bfloat16


def nn(a, b):
    return jnp.dot(a, b, preferred_element_type=F32)


def nt(a, b):
    return lax.dot_general(a, b, (((1,), (1,)), ((), ())), preferred_element_type=F32)


def tn(a, b):
    return lax.dot_general(a, b, (((0,), (0,)), ((), ())), preferred_element_type=F32)


def lanes(rows, width):
    return lax.broadcasted_iota(jnp.int32, (rows, width), 1)


def call(kernel, grid, in_specs, out_specs, out_shape, scratch, flops):
    return pl.pallas_call(
        kernel,
        grid=grid,
        in_specs=in_specs,
        out_specs=out_specs,
        out_shape=out_shape,
        scratch_shapes=scratch,
        compiler_params=pltpu.CompilerParams(
            vmem_limit_bytes=40 * 1024 * 1024, dimension_semantics=("arbitrary",)
        ),
        cost_estimate=pl.CostEstimate(flops=flops, bytes_accessed=flops // 512, transcendentals=0),
    )


def whole(shape):
    return pl.BlockSpec(shape, lambda p: (0,) * len(shape))


def columns(rows, start=0, row=0):
    return pl.BlockSpec((rows, 128), lambda p: (row, start + p))


def finish(copies):
    for copy in copies:
        copy.wait()


IN_VMEM = pl.BlockSpec(memory_space=pltpu.VMEM)
IN_PLACE = pl.BlockSpec(memory_space=pl.ANY)


def plain_call(kernel, in_specs, out_specs, out_shape, scratch, flops):
    return pl.pallas_call(
        kernel,
        grid=(1,),
        in_specs=in_specs,
        out_specs=out_specs,
        out_shape=out_shape,
        scratch_shapes=scratch,
        compiler_params=pltpu.CompilerParams(vmem_limit_bytes=48 * 1024 * 1024),
        cost_estimate=pl.CostEstimate(flops=flops, bytes_accessed=flops // 512, transcendentals=0),
    )


def rms_inverse(inputs):
    return lax.rsqrt(jnp.mean(inputs * inputs, axis=-1, keepdims=True) + epsilon)


def rms_forward(inputs, gain_row):
    return (inputs * rms_inverse(inputs) * gain_row).astype(BF16)


def rms_backward(inputs, gain_row, grad_normed):
    inverse = rms_inverse(inputs)
    scaled = grad_normed * gain_row
    grad_inputs = inverse * scaled - inputs * inverse**3 * jnp.mean(
        scaled * inputs, axis=-1, keepdims=True
    )
    grad_gain = jnp.sum(grad_normed * inputs * inverse, axis=0, keepdims=True)
    return grad_inputs, grad_gain


def pair_lanes(pair, start=0):
    return pl.ds(pl.multiple_of(start + pair * 128, 128), 128)


def stacked(value):
    lane = lanes(*value.shape)
    zero = jnp.zeros_like(value)
    return jnp.concatenate(
        [jnp.where(lane < 64, value, zero), jnp.where(lane < 64, zero, value)], axis=0
    )


def unstacked(value):
    rows = value.shape[0] // 2
    return jnp.where(lanes(rows, 128) < 64, value[:rows], value[rows:])


def twice(value, axis):
    return jnp.concatenate([value, value], axis=axis)


def taylor_mask(doc_t, doc_s, t_start, t_axis):
    t = t_start + lax.broadcasted_iota(jnp.int32, (doc_t == doc_s).shape, t_axis)
    s = lax.broadcasted_iota(jnp.int32, (doc_t == doc_s).shape, 1 - t_axis)
    return jnp.where((doc_t == doc_s) & (s <= t), 1.0, 0.0).astype(F32)


def taylor_queries(q, pair):
    wide = lanes(*q.shape) // FEAT_DIM
    zero = jnp.zeros_like(q)
    scaled = q * jnp.asarray(0.25, BF16)
    return jnp.concatenate(
        [jnp.where(wide == 2 * pair + i, scaled, zero) for i in range(2)], axis=0
    )


def taylor_forward_kernel(m, size, x_ref, gain_ref, docc, docr, in_ref, out_w_ref, *refs):
    earlier, refs = refs[:m], refs[m:]
    out_ref, kept_ref, mix_ref, den_ref, w_in, w_out, kv, mask, sems = refs
    rows = (m + 1) * size
    narrow, width = 2 * 128, x_ref.shape[1]
    cols = kept_ref.shape[1]
    reads = [
        pltpu.make_async_copy(
            in_ref.at[:, pl.ds(0, 2 * narrow)], w_in.at[:, pl.ds(0, 2 * narrow)], sems.at[0]
        ),
        pltpu.make_async_copy(
            in_ref.at[:, pl.ds(2 * narrow, width)], w_in.at[:, pl.ds(2 * narrow, width)], sems.at[1]
        ),
        pltpu.make_async_copy(out_w_ref.at[pl.ds(0, width), :], w_out, sems.at[2]),
    ] + [
        pltpu.make_async_copy(
            earlier[j].at[:, pl.ds(narrow, cols - narrow)],
            kv.at[pl.ds(j * size, size), :],
            sems.at[3 + j],
        )
        for j in range(m)
    ]
    for copy in reads:
        copy.start()
    inputs = x_ref[...].astype(F32)
    normed = rms_forward(inputs, gain_ref[...])
    mask[...] = taylor_mask(docc[m * size : rows, :], docr[:, :rows], m * size, 0)
    den_ref[...] = jnp.zeros_like(den_ref)
    reads[0].wait()
    kept_ref[:, : 2 * narrow] = nn(normed, w_in[:, : 2 * narrow]).astype(BF16)
    reads[1].wait()
    kept_ref[:, 2 * narrow :] = nn(normed, w_in[:, 2 * narrow :]).astype(BF16)
    kv[m * size : rows, :] = kept_ref[:, narrow:]
    finish(reads[3:])
    lane = lanes(size, 128)

    def one(pair, carry):
        a = nt(taylor_queries(kept_ref[:, :narrow], pair), kv[:, :narrow])
        w = (1.0 + a * (1.0 + 0.5 * a)) * twice(mask[...], 0)
        denom = jnp.sum(w, axis=1, keepdims=True)
        ratio = nn(w.astype(BF16), kv[:, pair_lanes(pair, narrow)]) / denom
        mix_ref[:, pair_lanes(pair)] = unstacked(ratio).astype(BF16)
        den_ref[...] = jnp.where(
            lane == 2 * pair,
            denom[:size],
            jnp.where(lane == 2 * pair + 1, denom[size:], den_ref[...]),
        )
        return carry

    lax.fori_loop(0, PAIRS, one, 0)
    reads[2].wait()
    out_ref[...] = (inputs + nn(mix_ref[...], w_out[...])).astype(BF16)


def taylor_forward(m, x, x_row, gain, docs, pack_in, pack_out, earlier):
    width = pack_in.shape[0]
    size = docs[0].shape[0] // CHUNKS
    cols = 2 * HEADS * FEAT_DIM + width
    low = jax.ShapeDtypeStruct((size, width), BF16)
    return plain_call(
        functools.partial(taylor_forward_kernel, m, size),
        [pl.BlockSpec((size, width), lambda p: (x_row, 0))] + [IN_VMEM] * 3 + [IN_PLACE] * (2 + m),
        [IN_VMEM] * 4,
        [
            low,
            jax.ShapeDtypeStruct((size, cols), BF16),
            low,
            jax.ShapeDtypeStruct((size, 128), F32),
        ],
        [
            pltpu.VMEM((width, cols), BF16),
            pltpu.VMEM((width, width), BF16),
            pltpu.VMEM(((m + 1) * size, cols - 256), BF16),
            pltpu.VMEM((size, (m + 1) * size), F32),
            pltpu.SemaphoreType.DMA((3 + m,)),
        ],
        2 * size * width * (cols + width),
    )(x, gain, *docs[:2], pack_in, pack_out, *earlier)


def taylor_backward_kernel(m, size, later, *refs):
    docc, docr, q_ref = refs[:3]
    refs = refs[3:]
    ks, vs = refs[: m + 1], refs[m + 1 : 2 * m + 2]
    dmix_ref, mix_ref, den_ref = refs[2 * m + 2 : 2 * m + 5]
    refs = refs[2 * m + 5 :]
    if later:
        dk_in, dv_in = refs[:2]
        refs = refs[2:]
    dq_ref, dk_ref, dv_ref, mask, k_all, k_turned, dq_turned = refs
    pair = pl.program_id(0)
    rows = (m + 1) * size

    @pl.when(pair == 0)
    def _():
        mask[...] = taylor_mask(docr[:, m * size : rows], docc[:rows, :], m * size, 1)
        for j in range(m + 1):
            k = ks[j][...]
            k_all[j * size : (j + 1) * size, :] = k
            k_turned[:, j * size : (j + 1) * size] = (k.astype(F32) * 0.25).T.astype(BF16)
        dk_ref[...] = jnp.zeros_like(dk_ref)
        if later:
            dk_ref[: m * size, :] = dk_in[...]

    lane = lanes(size, 128)
    dm = dmix_ref[...].astype(F32)
    both = dm * mix_ref[...].astype(F32)
    dnums, extras = [], []
    for i in range(2):
        inside = lane // 64 == i
        turn = 1.0 / jnp.sum(
            jnp.where(lane == 2 * pair + i, den_ref[...], 0.0), axis=1, keepdims=True
        )
        dden = -jnp.sum(jnp.where(inside, both, 0.0), axis=1, keepdims=True) * turn
        high = dden.astype(BF16).astype(F32)
        dnums.append(jnp.where(inside, dm * turn, 0.0).astype(BF16))
        extras.append(
            jnp.where(lane == 0, high, jnp.where(lane == 1, dden - high, 0.0)).astype(BF16)
        )
    dnum = jnp.concatenate(dnums, axis=0)
    dnum_more = jnp.concatenate([dnum, jnp.concatenate(extras, axis=0)], axis=1)
    q = taylor_queries(q_ref[...], pair)
    v = jnp.concatenate([part[...] for part in vs], axis=0)
    a = nt(k_all[...], q)
    masks = twice(mask[...], 1)
    w = (1.0 + a * (1.0 + 0.5 * a)) * masks
    dw = nt(jnp.concatenate([v, jnp.ones_like(v)], axis=1), dnum_more)
    da = (dw * (1.0 + a) * masks).astype(BF16)
    dv = nn(w.astype(BF16), dnum)
    if later:
        dv_ref[: m * size, :] = dv_in[...] + dv[: m * size]
        dv_ref[m * size :, :] = dv[m * size :]
    else:
        dv_ref[...] = dv
    dk_ref[...] += nn(da, q)
    own = pl.ds(pl.multiple_of(pair * 2 * FEAT_DIM, 2 * FEAT_DIM), 2 * FEAT_DIM)
    dq = nn(k_turned[own, :], da)
    dq_turned[own, :] = jnp.concatenate([dq[:FEAT_DIM, :size], dq[FEAT_DIM:, size:]], axis=0)

    @pl.when(pair == PAIRS - 1)
    def _():
        dq_ref[...] = dq_turned[...].T


def taylor_backward(m, docs, kept, dmix, mix, den, later):
    size = kept[0].shape[0]
    docc, docr = docs[:2]
    rows = (m + 1) * size
    return call(
        functools.partial(taylor_backward_kernel, m, size, later is not None),
        (PAIRS,),
        [whole(docc.shape), whole(docr.shape), whole((size, 256))]
        + [pl.BlockSpec((size, 256), lambda p: (0, 1))] * (m + 1)
        + [columns(size, 4)] * (m + 1)
        + [columns(size), columns(size), whole((size, 128))]
        + ([whole((m * size, 256)), columns(m * size)] if later is not None else []),
        [whole((size, 256)), whole((rows, 256)), columns(rows)],
        [
            jax.ShapeDtypeStruct((size, 256), F32),
            jax.ShapeDtypeStruct((rows, 256), F32),
            jax.ShapeDtypeStruct((rows, HEADS * 64), F32),
        ],
        [
            pltpu.VMEM((rows, size), F32),
            pltpu.VMEM((rows, 256), BF16),
            pltpu.VMEM((256, rows), BF16),
            pltpu.VMEM((256, size), F32),
        ],
        5 * HEADS * (m + 1) * size * size * 512,
    )(docc, docr, kept[m], *kept, *kept, dmix, mix, den, *(later or ()))


STEP = 128
UNROLL = 4


def window_docs(docs):
    return jnp.concatenate([jnp.full((STEP,), -1, jnp.int32), docs])[:, None]


def window_biases(m, size, docc, docr, bias):
    s = lax.broadcasted_iota(jnp.int32, (2 * STEP, STEP), 0)
    t = STEP + lax.broadcasted_iota(jnp.int32, (2 * STEP, STEP), 1)
    near = (t >= s) & (t - s < WINDOW)
    for b in range(size // STEP):
        at = m * size + b * STEP
        same = docr[:, at : at + STEP] == docc[at : at + 2 * STEP, :]
        bias[b] = jnp.where(near & same, 0.0, -1e30).astype(F32)


def window_weights(k, q, bias):
    a = nt(k, q) + twice(bias, 1)
    p = jnp.exp(a - jnp.max(a, axis=0, keepdims=True))
    return p * (1.0 / jnp.sum(p, axis=0, keepdims=True))


def joined(before, own, cut):
    value = own[:, cut]
    first = before[:, cut] if before is not None else jnp.zeros((STEP, 128), BF16)
    return jnp.concatenate([first, value], axis=0)


def window_forward_kernel(m, size, x_ref, gain_ref, docc, docr, in_ref, out_w_ref, *refs):
    before, refs = (refs[0], refs[1:]) if m > 0 else (None, refs)
    out_ref, kept_ref, mix_ref, w_in, w_out, bias, sems = refs
    width = x_ref.shape[1]
    reads = [
        pltpu.make_async_copy(
            in_ref.at[:, pl.ds(i * width, width)], w_in.at[:, pl.ds(i * width, width)], sems.at[i]
        )
        for i in range(3)
    ] + [pltpu.make_async_copy(out_w_ref.at[pl.ds(0, width), :], w_out, sems.at[3])]
    for copy in reads:
        copy.start()
    inputs = x_ref[...].astype(F32)
    normed = rms_forward(inputs, gain_ref[...])
    for i in range(3):
        cut = slice(i * width, (i + 1) * width)
        reads[i].wait()
        kept_ref[:, cut] = nn(normed, w_in[:, cut]).astype(BF16)

    window_biases(m, size, docc, docr, bias)

    def one(pair, carry):
        cuts = [pair_lanes(pair, i * width) for i in range(3)]
        k_all = joined(before, kept_ref, cuts[1])
        v_all = joined(before, kept_ref, cuts[2])
        for b in range(size // STEP):
            own = slice(b * STEP, (b + 1) * STEP)
            keys = slice(b * STEP, (b + 2) * STEP)
            q = stacked(kept_ref[own, cuts[0]] * jnp.asarray(0.125, BF16))
            p = window_weights(k_all[keys], q, bias[b])
            mix_ref[own, cuts[0]] = unstacked(tn(p.astype(BF16), v_all[keys])).astype(BF16)
        return carry

    lax.fori_loop(0, PAIRS, one, 0, unroll=UNROLL)
    reads[3].wait()
    out_ref[...] = (inputs + nn(mix_ref[...], w_out[...])).astype(BF16)


def before_spec(size, cols):
    return pl.BlockSpec((STEP, cols), lambda p: (size // STEP - 1, 0))


def window_forward(m, x, gain, docs, pack_in, pack_out, before):
    size, width = x.shape
    low = jax.ShapeDtypeStruct((size, width), BF16)
    more = [before_spec(size, 3 * width)] if m > 0 else []
    return plain_call(
        functools.partial(window_forward_kernel, m, size),
        [IN_VMEM] * 4 + [IN_PLACE] * 2 + more,
        [IN_VMEM] * 3,
        [low, jax.ShapeDtypeStruct((size, 3 * width), BF16), low],
        [
            pltpu.VMEM((width, 3 * width), BF16),
            pltpu.VMEM((width, width), BF16),
            pltpu.VMEM((size // STEP, 2 * STEP, STEP), F32),
            pltpu.SemaphoreType.DMA((4,)),
        ],
        8 * size * width * width,
    )(x, gain, docs[2], docs[1], pack_in, pack_out, *([before] if m > 0 else []))


def window_backward_kernel(m, size, docc, docr, kept_ref, g_ref, out_w_ref, *refs):
    w_out, dmix, bias, sems = refs[-4:]
    refs = refs[:-4]
    before = None
    if m > 0:
        before, part_ref, x_ref, gain_ref, g_before_ref, in_ref = refs[:6]
        grad_ref, out_ref, done_ref, dgain_ref, w_in = refs[6:]
    else:
        (grad_ref,) = refs
    width = g_ref.shape[1]
    first = pltpu.make_async_copy(out_w_ref.at[pl.ds(0, width), :], w_out, sems.at[3])
    first.start()
    reads = []
    if m > 0:
        reads = [
            pltpu.make_async_copy(
                in_ref.at[:, pl.ds(i * width, width)],
                w_in.at[:, pl.ds(i * width, width)],
                sems.at[i],
            )
            for i in range(3)
        ]
        for copy in reads:
            copy.start()
        done_ref[...] = part_ref[...]
    first.wait()
    dmix[...] = nt(g_ref[...], w_out[...]).astype(BF16)

    window_biases(m, size, docc, docr, bias)

    def one(pair, carry):
        cuts = [pair_lanes(pair, i * width) for i in range(3)]
        k_all = joined(before, kept_ref, cuts[1])
        v_all = joined(before, kept_ref, cuts[2])
        blocks = size // STEP
        halves = [[0.0] * (blocks + 1) for _ in range(2)]
        for b in range(blocks):
            own = slice(b * STEP, (b + 1) * STEP)
            keys = slice(b * STEP, (b + 2) * STEP)
            q = stacked(kept_ref[own, cuts[0]] * jnp.asarray(0.125, BF16))
            dm = stacked(dmix[own, cuts[0]])
            k, v = k_all[keys], v_all[keys]
            p = window_weights(k, q, bias[b])
            dp = nt(v, dm)
            da = (p * (dp - jnp.sum(p * dp, axis=0, keepdims=True))).astype(BF16)
            for half, more in zip(halves, (nn(da, q), nn(p.astype(BF16), dm))):
                half[b] = half[b] + more[:STEP]
                half[b + 1] = more[STEP:]
            dq = unstacked(tn(da, k * jnp.asarray(0.125, BF16)))
            grad_ref[own, cuts[0]] = dq.astype(BF16)
        for half, cut in zip(halves, cuts[1:]):
            grad_ref[:, cut] = jnp.concatenate(half[1:], axis=0).astype(BF16)
            if m > 0:
                tail = slice(size - STEP, size)
                done_ref[tail, cut] = (part_ref[tail, cut].astype(F32) + half[0]).astype(BF16)
        return carry

    lax.fori_loop(0, PAIRS, one, 0, unroll=UNROLL)
    if m > 0:
        total = 0.0
        for i in range(3):
            cut = slice(i * width, (i + 1) * width)
            reads[i].wait()
            total = total + nt(done_ref[:, cut], w_in[:, cut])
        grad, dgain = rms_backward(x_ref[...].astype(F32), gain_ref[...], total)
        out_ref[...] = (g_before_ref[...].astype(F32) + grad).astype(BF16)
        dgain_ref[...] = dgain


def window_backward(m, docs, kept, g, pack_out, before, settle):
    size, width = g.shape
    low = jax.ShapeDtypeStruct((size, width), BF16)
    wide = jax.ShapeDtypeStruct((size, 3 * width), BF16)
    more, arrays = [], []
    if m > 0:
        more = [before_spec(size, 3 * width)] + [IN_VMEM] * 4 + [IN_PLACE]
        arrays = [before, *settle]
    return plain_call(
        functools.partial(window_backward_kernel, m, size),
        [IN_VMEM] * 4 + [IN_PLACE] + more,
        [IN_VMEM] * (4 if m > 0 else 1),
        [wide] + ([low, wide, jax.ShapeDtypeStruct((1, width), F32)] if m > 0 else []),
        ([pltpu.VMEM((width, 3 * width), BF16)] if m > 0 else [])
        + [
            pltpu.VMEM((width, width), BF16),
            pltpu.VMEM((size, width), BF16),
            pltpu.VMEM((size // STEP, 2 * STEP, STEP), F32),
            pltpu.SemaphoreType.DMA((4,)),
        ],
        16 * size * width * width,
    )(docs[2], docs[1], kept, g, pack_out, *arrays)


def blank(shapes):
    return pl.pallas_call(
        lambda *refs: None,
        out_specs=[pl.BlockSpec(memory_space=pl.ANY)] * len(shapes),
        out_shape=[jax.ShapeDtypeStruct(*shape) for shape in shapes],
    )()


def spans(width):
    return (2, width // 2) if width % 256 == 0 else (1, width)


def tile_copies(refs, sems, n, w):
    at = pl.ds(pl.multiple_of(n * w, 128), w)
    made = []
    for i, (a, b, axis) in enumerate(refs):
        cut = (at, slice(None)) if axis == 0 else (slice(None), at)
        made.append(pltpu.make_async_copy(a.at[cut], b.at[cut], sems.at[n, i]))
    return made


def start_all(refs, sems, count, w):
    for n in range(count):
        for copy in tile_copies(refs, sems, n, w):
            copy.start()


def out_copies(wo_ref, wo, sems, count, w):
    rows = wo_ref.shape[0]
    if wo.shape[0] > rows:
        wo[rows:, :] = jnp.zeros((wo.shape[0] - rows, wo.shape[1]), BF16)
    made = []
    for n in range(count):
        cut = pl.ds(n * w, min(w, rows - n * w))
        made.append(pltpu.make_async_copy(wo_ref.at[cut, :], wo.at[cut, :], sems.at[n]))
    return made


def wait_for(copies, n):
    for i, copy in enumerate(copies):
        pl.when(n == i)(copy.wait)


def dense_forward_kernel(
    x_ref,
    gain_ref,
    wg_ref,
    wu_ref,
    wo_ref,
    out_ref,
    gate_ref,
    up_ref,
    wg,
    wu,
    wo,
    gates,
    ups,
    normed,
    total,
    sems,
    out_sems,
    done,
):
    count, w = spans(gates.shape[1])
    reads = [(wg_ref, wg, 1), (wu_ref, wu, 1)]
    writes = [(gates, gate_ref, 1), (ups, up_ref, 1)]
    start_all(reads, sems, count, w)
    outs = out_copies(wo_ref, wo, out_sems, count, w)
    for copy in outs:
        copy.start()
    inputs = x_ref[...].astype(F32)
    normed[...] = rms_forward(inputs, gain_ref[...])
    total[...] = inputs

    def tile(n, carry):
        cut = pl.ds(pl.multiple_of(n * w, 128), w)
        came = tile_copies(reads, sems, n, w)
        came[0].wait()
        gate = nn(normed[...], wg[:, cut])
        came[1].wait()
        up = nn(normed[...], wu[:, cut])
        gates[:, cut] = gate.astype(BF16)
        ups[:, cut] = up.astype(BF16)
        for copy in tile_copies(writes, done, n, w):
            copy.start()
        hidden = (gate * jax.nn.sigmoid(gate) * up).astype(BF16)
        wait_for(outs, n)
        total[...] += nn(hidden, wo[cut, :])
        return carry

    lax.fori_loop(0, count, tile, 0)
    out_ref[...] = total[...].astype(BF16)
    for n in range(count):
        finish(tile_copies(writes, done, n, w))


def weight_scratch(width, padded):
    return [pltpu.VMEM((width, padded), BF16)] * 2 + [pltpu.VMEM((padded, width), BF16)]


def dense_forward(x, gain, weights):
    size, width = x.shape
    padded = weights[1].shape[1]
    tiles = spans(padded)[0]
    return plain_call(
        dense_forward_kernel,
        [IN_VMEM, IN_VMEM] + [IN_PLACE] * 3,
        [IN_VMEM, IN_PLACE, IN_PLACE],
        [jax.ShapeDtypeStruct((size, width), BF16)]
        + [jax.ShapeDtypeStruct((size, padded), BF16)] * 2,
        weight_scratch(width, padded)
        + [pltpu.VMEM((size, padded), BF16)] * 2
        + [pltpu.VMEM((size, width), BF16), pltpu.VMEM((size, width), F32)]
        + [pltpu.SemaphoreType.DMA(shape) for shape in ((tiles, 2), (tiles,), (tiles, 2))],
        6 * size * width * padded,
    )(x, gain, *weights)


def dense_backward_kernel(
    x_ref,
    gain_ref,
    g_ref,
    gate_ref,
    up_ref,
    wg_ref,
    wu_ref,
    wo_ref,
    out_ref,
    dgate_ref,
    dup_ref,
    hidden_ref,
    dgain_ref,
    wg,
    wu,
    wo,
    gates,
    ups,
    dgates,
    dups,
    hiddens,
    total,
    sems,
    out_sems,
    done,
):
    count, w = spans(gates.shape[1])
    reads = [(gate_ref, gates, 1), (up_ref, ups, 1), (wg_ref, wg, 1), (wu_ref, wu, 1)]
    writes = [(hiddens, hidden_ref, 1), (dgates, dgate_ref, 1), (dups, dup_ref, 1)]
    outs = out_copies(wo_ref, wo, out_sems, count, w)
    for copy in outs:
        copy.start()
    start_all(reads, sems, count, w)
    total[...] = jnp.zeros_like(total)

    def tile(n, carry):
        cut = pl.ds(pl.multiple_of(n * w, 128), w)
        came = tile_copies(reads, sems, n, w)
        wait_for(outs, n)
        finish(came[:2])
        dh = nt(g_ref[...], wo[cut, :])
        gate = gates[:, cut].astype(F32)
        up = ups[:, cut].astype(F32)
        sg = jax.nn.sigmoid(gate)
        active = gate * sg
        hiddens[:, cut] = (active * up).astype(BF16)
        dgate = (dh * up * (sg + active * (1.0 - sg))).astype(BF16)
        dup = (dh * active).astype(BF16)
        dgates[:, cut] = dgate
        dups[:, cut] = dup
        for copy in tile_copies(writes, done, n, w):
            copy.start()
        finish(came[2:])
        total[...] += nt(dgate, wg[:, cut]) + nt(dup, wu[:, cut])
        return carry

    lax.fori_loop(0, count, tile, 0)
    grad, dgain = rms_backward(x_ref[...].astype(F32), gain_ref[...], total[...])
    out_ref[...] = (g_ref[...].astype(F32) + grad).astype(BF16)
    dgain_ref[...] = dgain
    for n in range(count):
        finish(tile_copies(writes, done, n, w))


def dense_backward(x, gain, g, gate, up, weights):
    size, width = x.shape
    padded = weights[1].shape[1]
    tiles = spans(padded)[0]
    return plain_call(
        dense_backward_kernel,
        [IN_VMEM] * 3 + [IN_PLACE] * 5,
        [IN_VMEM] + [IN_PLACE] * 3 + [IN_VMEM],
        [jax.ShapeDtypeStruct((size, width), BF16)]
        + [jax.ShapeDtypeStruct((size, padded), BF16)] * 3
        + [jax.ShapeDtypeStruct((1, width), F32)],
        weight_scratch(width, padded)
        + [pltpu.VMEM((size, padded), BF16)] * 5
        + [pltpu.VMEM((size, width), F32)]
        + [pltpu.SemaphoreType.DMA(shape) for shape in ((tiles, 4), (tiles,), (tiles, 3))],
        6 * size * width * padded,
    )(x, gain, g, gate, up, *weights)


def dense_both_kernel(
    x_ref,
    gain_ref,
    g_ref,
    wg_ref,
    wu_ref,
    wo_ref,
    final_ref,
    out_ref,
    dgate_ref,
    dup_ref,
    hidden_ref,
    dgain_ref,
    wg,
    wu,
    wo,
    dgates,
    dups,
    hiddens,
    normed,
    final,
    total,
    sems,
    out_sems,
    done,
):
    count, w = spans(dgates.shape[1])
    reads = [(wg_ref, wg, 1), (wu_ref, wu, 1)]
    writes = [(hiddens, hidden_ref, 1), (dgates, dgate_ref, 1), (dups, dup_ref, 1)]
    start_all(reads, sems, count, w)
    outs = out_copies(wo_ref, wo, out_sems, count, w)
    for copy in outs:
        copy.start()
    inputs = x_ref[...].astype(F32)
    normed[...] = rms_forward(inputs, gain_ref[...])
    final[...] = inputs
    total[...] = jnp.zeros_like(total)

    def tile(n, carry):
        cut = pl.ds(pl.multiple_of(n * w, 128), w)
        came = tile_copies(reads, sems, n, w)
        came[0].wait()
        gate = nn(normed[...], wg[:, cut])
        came[1].wait()
        up = nn(normed[...], wu[:, cut])
        sg = jax.nn.sigmoid(gate)
        active = gate * sg
        hidden = (active * up).astype(BF16)
        hiddens[:, cut] = hidden
        wait_for(outs, n)
        final[...] += nn(hidden, wo[cut, :])
        dh = nt(g_ref[...], wo[cut, :])
        dgate = (dh * up * (sg + active * (1.0 - sg))).astype(BF16)
        dup = (dh * active).astype(BF16)
        dgates[:, cut] = dgate
        dups[:, cut] = dup
        for copy in tile_copies(writes, done, n, w):
            copy.start()
        total[...] += nt(dgate, wg[:, cut]) + nt(dup, wu[:, cut])
        return carry

    lax.fori_loop(0, count, tile, 0)
    final_ref[...] = final[...].astype(BF16)
    grad, dgain = rms_backward(inputs, gain_ref[...], total[...])
    out_ref[...] = (g_ref[...].astype(F32) + grad).astype(BF16)
    dgain_ref[...] = dgain
    for n in range(count):
        finish(tile_copies(writes, done, n, w))


def dense_both(x, gain, g, weights):
    size, width = x.shape
    padded = weights[1].shape[1]
    tiles = spans(padded)[0]
    return plain_call(
        dense_both_kernel,
        [IN_VMEM] * 3 + [IN_PLACE] * 3,
        [IN_VMEM] * 2 + [IN_PLACE] * 3 + [IN_VMEM],
        [jax.ShapeDtypeStruct((size, width), BF16)] * 2
        + [jax.ShapeDtypeStruct((size, padded), BF16)] * 3
        + [jax.ShapeDtypeStruct((1, width), F32)],
        weight_scratch(width, padded)
        + [pltpu.VMEM((size, padded), BF16)] * 3
        + [pltpu.VMEM((size, width), BF16)]
        + [pltpu.VMEM((size, width), F32)] * 2
        + [pltpu.SemaphoreType.DMA(shape) for shape in ((tiles, 2), (tiles,), (tiles, 3))],
        12 * size * width * padded,
    )(x, gain, g, *weights)


def grad_in_kernel(count, tiles, gain_ref, *refs):
    xs, refs = refs[:count], refs[count:]
    groups = [refs[count * n : count * (n + 1)] for n in range(len(tiles))]
    out_ref, turned = refs[count * len(tiles) :]
    step = pl.program_id(0)
    size = xs[0].shape[0]

    @pl.when(step == 0)
    def _():
        for c in range(count):
            normed = rms_forward(xs[c][...].astype(F32), gain_ref[...])
            turned[:, c * size : (c + 1) * size] = normed.astype(F32).T.astype(BF16)

    start = 0
    for parts, (_, used) in zip(groups, tiles):

        @pl.when((step >= start) & (step < start + used))
        def _(parts=parts):
            joined = jnp.concatenate([part[...] for part in parts], axis=0)
            out_ref[...] = nn(turned[...], joined).astype(BF16)

        start += used


def grad_in(gain, xs, groups, out_width, tile):
    count = len(xs)
    size, width = xs[0].shape
    specs = [whole((1, width))] + [whole((size, width))] * count
    arrays, begun = [], 0
    for parts, first, used in groups:

        def at(j, first=first, used=used, begun=begun):
            return (0, first + jnp.clip(j - begun, 0, used - 1))

        specs += [pl.BlockSpec((size, tile), at)] * count
        arrays += parts
        begun += used
    return call(
        functools.partial(grad_in_kernel, count, [group[1:] for group in groups]),
        (begun,),
        specs,
        pl.BlockSpec((width, tile), lambda j: (0, j)),
        jax.ShapeDtypeStruct((width, out_width), BF16),
        [pltpu.VMEM((width, count * size), BF16)],
        2 * count * size * width * tile * begun,
    )(gain, *xs, *arrays)


def grad_out_kernel(count, used, *refs):
    left, right = refs[:count], refs[count : 2 * count]
    out_ref = refs[2 * count]
    step = pl.program_id(0)

    @pl.when(step < used)
    def _():
        joined = jnp.concatenate([part[...] for part in left], axis=0)
        turned = joined.astype(F32).T.astype(BF16)
        out_ref[...] = nn(turned, jnp.concatenate([part[...] for part in right], axis=0)).astype(
            BF16
        )

    @pl.when(step >= used)
    def _():
        out_ref[...] = jnp.zeros_like(out_ref)


def grad_out(left, right, used, rows):
    count = len(left)
    size, width = right[0].shape
    tiles = -(-rows // TILE)
    return call(
        functools.partial(grad_out_kernel, count, used),
        (tiles,),
        [pl.BlockSpec((size, TILE), lambda j: (0, jnp.minimum(j, used - 1)))] * count
        + [whole((size, width))] * count,
        pl.BlockSpec((TILE, width), lambda j: (j, 0)),
        jax.ShapeDtypeStruct((rows, width), BF16),
        [],
        2 * count * size * width * TILE * used,
    )(*left, *right)


def local(tokens, section_in, section_out, gains, bounds, cotangent):
    section = lax.axis_index("section")
    seq = lax.axis_index("seq")
    sections = lax.axis_size("section")
    pack_in = section_in[0]
    pack_out = section_out[0]
    gain_row = gains
    _, block, width = tokens.shape
    hidden_dim = pack_out.shape[0]
    padded = -(-hidden_dim // TILE) * TILE
    length = 2 * block
    size = length // CHUNKS
    taylor_cols = 2 * HEADS * FEAT_DIM + width
    window_cols = 3 * width
    last = sections - 1

    def swapped(two):
        away = lax.dynamic_index_in_dim(two, 1 - seq, 0, keepdims=False)
        own = lax.dynamic_index_in_dim(two, seq, 0, keepdims=False)
        came = lax.ppermute(away, "seq", [(0, 1), (1, 0)])
        return jnp.where(seq == 0, jnp.stack([own, came]), jnp.stack([came, own]))

    def branches(shapes, makers):
        names = list(shapes)

        def branch(maker):
            def run():
                made = maker() if maker is not None else {}
                missing = [name for name in names if name not in made]
                empty = dict(zip(missing, blank([shapes[name] for name in missing]))) if missing else {}
                return tuple(made[name] if name in made else empty[name] for name in names)

            return run

        values = lax.switch(section, [branch(maker) for maker in makers])
        return dict(zip(names, values))

    starts = lax.dynamic_index_in_dim(bounds, seq, 0, keepdims=False)
    positions = jnp.arange(length, dtype=jnp.int32)
    docs = jnp.sum((starts[None, :] <= positions[:, None]).astype(jnp.int32), axis=1)
    docs = (docs[:, None], docs[None, :], window_docs(docs))

    feed = swapped(jnp.where(section == 0, tokens, cotangent)).reshape(length, width)

    def fed(m):
        return feed[m * size : (m + 1) * size]

    first_back = (last + 1) * LAG
    turns = first_back + LAG + CHUNKS + 1
    low = ((size, width), BF16)
    wide = ((size, padded), BF16)
    gain_shape = ((1, width), F32)
    made, sent = [], []

    def prepare():
        up = pack_in[:, hidden_dim:]
        return {"wu": jnp.pad(up, ((0, 0), (0, padded - hidden_dim)))}

    def entry(s, m):
        return fed(m) if s == 0 else sent[m + LAG * (s - 1)]["out"]

    def upstream(s, m):
        if s == last:
            return fed(m)
        if s == 2:
            return sent[m + LAG * last]["out"]
        return sent[first_back + 1 + LAG * (1 - s) + m]["out"]

    def taylor_turn(m):
        def run():
            earlier = [made[i]["linear"] for i in range(m)]
            out, projected, mix, den = taylor_forward(
                m, feed, m, gain_row, docs, pack_in, pack_out, earlier
            )
            return {"out": out, "linear": projected, "mix": mix, "den": den}

        return run

    def dense_turn(m):
        def run():
            out, gate, up = dense_forward(entry(1, m), gain_row, weights)
            return {"out": out, "gate": gate, "up": up}

        return run

    def window_turn(m):
        def run():
            before = made[2 * LAG + m - 1]["window"] if m > 0 else None
            out, projected, mix = window_forward(
                m, entry(2, m), gain_row, docs, pack_in, pack_out, before
            )
            return {"out": out, "window": projected, "mix": mix}

        return run

    def dense_both_turn(m):
        def run():
            final, out, dgate, dup, hidden, gain = dense_both(
                entry(3, m), gain_row, upstream(3, m), weights
            )
            return {
                "final": final,
                "out": out,
                "dgate": dgate,
                "dup": dup,
                "hidden": hidden,
                "gain": gain,
            }

        return run

    def window_back(m):
        def run():
            if m == CHUNKS:
                done = made[first_back + m - 1]["part"]
                grad, gain = rms_backward(
                    entry(2, m - 1).astype(F32), gain_row, nt(done, pack_in[:, :window_cols])
                )
                out = (upstream(2, m - 1).astype(F32) + grad).astype(BF16)
                return {"out": out, "done": done, "gain": gain}
            before = made[2 * LAG + m - 1]["window"] if m > 0 else None
            settle = ()
            if m > 0:
                settle = (
                    made[first_back + m - 1]["part"],
                    entry(2, m - 1),
                    gain_row,
                    upstream(2, m - 1),
                    pack_in,
                )
            results = window_backward(
                m, docs, made[2 * LAG + m]["window"], upstream(2, m), pack_out, before, settle
            )
            values = {"part": results[0]}
            if m > 0:
                values.update(out=results[1], done=results[2], gain=results[3])
            return values

        return run

    def dense_back(m):
        def run():
            kept = made[LAG + m]
            out, dgate, dup, hidden, gain = dense_backward(
                entry(1, m), gain_row, upstream(1, m), kept["gate"], kept["up"], weights
            )
            return {"out": out, "dgate": dgate, "dup": dup, "hidden": hidden, "gain": gain}

        return run

    def taylor_back(ms, earlier):
        dqs = []
        for m in ms:
            dmix = nt(upstream(0, m), pack_out[:width]).astype(BF16)
            dq, dk, dv = taylor_backward(
                m,
                docs,
                [made[i]["linear"] for i in range(m + 1)],
                dmix,
                made[m]["mix"],
                made[m]["den"],
                earlier,
            )
            earlier = (dk, dv)
            dqs.append(dq)
        return dqs, earlier

    def taylor_turn_back(m):
        def run():
            earlier = (made[-1]["dk"], made[-1]["dv"]) if m > 0 else None
            dqs, (dk, dv) = taylor_back([m], earlier)
            return {"dq": dqs[0], "dk": dk, "dv": dv}

        return run

    def spread(two, source):
        share = width // sections
        mine = two[:, :, source * share : (source + 1) * share]
        for target in range(sections):
            if target != source:
                piece = two[:, :, target * share : (target + 1) * share]
                came = lax.ppermute(piece, "section", [(source, target)])
                mine = jnp.where(section == target, came, mine)
        return mine

    taylor_shapes = {}
    for t in range(turns + 1):
        shapes, makers, pairs = {}, [None] * sections, []
        for s in range(sections):
            m = t - LAG * s
            if 0 <= m < CHUNKS:
                shapes["out"] = low
                makers[s] = (taylor_turn, dense_turn, window_turn, dense_both_turn)[s](m)
                if s == 0:
                    shapes.update(linear=((size, taylor_cols), BF16), mix=low)
                    shapes["den"] = ((size, 128), F32)
                elif s == 1:
                    shapes.update(gate=wide, up=wide)
                elif s == 2:
                    shapes.update(window=((size, window_cols), BF16), mix=low)
                else:
                    shapes.update(final=low, dgate=wide, dup=wide, hidden=wide, gain=gain_shape)
                pairs.append((s, s + 1) if s < last else (s, s - 1))
        if t == 0:
            shapes["wu"] = ((width, padded), BF16)
            makers[1] = makers[3] = prepare
        m = t - first_back
        if 0 <= m <= CHUNKS:
            makers[2] = window_back(m)
            if m < CHUNKS:
                shapes["part"] = ((size, window_cols), BF16)
            if m > 0:
                shapes.update(out=low, done=((size, window_cols), BF16), gain=gain_shape)
                pairs.append((2, 1))
        m = t - first_back - 1 - LAG
        if 0 <= m < CHUNKS:
            makers[1] = dense_back(m)
            shapes.update(out=low, dgate=wide, dup=wide, hidden=wide, gain=gain_shape)
            pairs.append((1, 0))
        m = t - first_back - 1 - 2 * LAG
        if 0 <= m < CHUNKS - 1:
            makers[0] = taylor_turn_back(m)
            rows = (m + 1) * size
            taylor_shapes = {
                "dq": ((size, 256), F32),
                "dk": ((rows, 256), F32),
                "dv": ((rows, width), F32),
            }
            shapes.update(taylor_shapes)
        if t == turns:
            break
        made.append(branches(shapes, makers))
        if t == 0:
            weights = (pack_in, made[0]["wu"], pack_out)
        sent.append({"out": lax.ppermute(made[t]["out"], "section", pairs)} if pairs else {})

    def turns_of(s):
        start = (0, first_back + 1 + LAG, first_back + 1, LAG * last)[s]
        return made[start : start + CHUNKS]

    def every(s, name):
        return [value[name] for value in turns_of(s)]

    def gains_of(s):
        return sum(value["gain"] for value in turns_of(s))

    def entries(s):
        return [entry(s, m) for m in range(CHUNKS)]

    def upstreams(s):
        return [upstream(s, m) for m in range(CHUNKS)]

    half = padded // 2
    b_cols = max(taylor_cols, half)
    owners = lax.axis_size("dp") * lax.axis_size("seq")
    a_cols = 3 * half
    a_shape = ((width, a_cols), BF16)
    fold = width // owners
    rest_rows = fold * b_cols // width + hidden_dim // owners
    rest_shape = ((owners, rest_rows, width), BF16)

    def folded(b, c):
        b = b.reshape(owners, fold, b_cols)
        parts = [b[:, :, :width]]
        extra = b_cols - width
        count = width // extra
        step = fold // count
        parts.append(
            jnp.concatenate(
                [b[:, i * step : (i + 1) * step, width:] for i in range(count)], axis=2
            )
        )
        return {"rest": jnp.concatenate(parts + [c.reshape(owners, -1, width)], axis=1)}

    def unfolded(rows):
        extra = b_cols - width
        step = fold * extra // width
        more = rows[fold : fold + step]
        right = jnp.concatenate(
            [more[:, i * extra : (i + 1) * extra] for i in range(width // extra)], axis=0
        )
        return jnp.concatenate([rows[:fold], right], axis=1), rows[fold + step :]

    def dense_first(s):
        def run():
            groups = [(every(s, "dgate"), 0, 2), (every(s, "dup"), 0, 1)]
            return {"a": grad_in(gain_row, entries(s), groups, a_cols, half)}

        return run

    def window_first():
        groups = [(every(2, "done"), 0, 3)]
        return {"a": grad_in(gain_row, entries(2), groups, a_cols, window_cols // 3)}

    def dense_second(s):
        def run():
            groups = [(every(s, "dup"), 1, 1)]
            return folded(
                grad_in(gain_row, entries(s), groups, b_cols, half),
                grad_out(every(s, "hidden"), upstreams(s), padded // TILE, hidden_dim),
            )

        return run

    def window_second():
        mixes = [made[2 * LAG + m]["mix"] for m in range(CHUNKS)]
        (unused,) = blank([((width, b_cols), BF16)])
        return folded(unused, grad_out(mixes, upstreams(2), width // TILE, hidden_dim))

    def taylor_last():
        done = CHUNKS - 1
        dqs, (dk, dv) = taylor_back([done], (made[turns]["dk"], made[turns]["dv"]))
        dqs = [made[turns - done + 1 + m]["dq"] for m in range(done)] + dqs
        grad = jnp.concatenate([jnp.concatenate(dqs, axis=0), dk, dv], axis=1).astype(BF16)
        parts = folded(
            grad_in(gain_row, [feed], [([grad], 0, 2)], b_cols, taylor_cols // 2),
            grad_out(
                [made[m]["mix"] for m in range(CHUNKS)], upstreams(0), width // TILE, hidden_dim
            ),
        )
        return {"linear": grad, **parts}

    def taylor_final():
        came = jnp.concatenate(upstreams(0), axis=0)
        grad_inputs, gain = rms_backward(
            feed.astype(F32), gain_row, nt(rest["linear"], pack_in[:, :taylor_cols])
        )
        return {"returned": (came.astype(F32) + grad_inputs).astype(BF16), "gain": gain}

    made.append(
        branches(
            {"a": a_shape, **taylor_shapes},
            [taylor_turn_back(CHUNKS - 2), dense_first(1), window_first, dense_first(3)],
        )
    )
    axes = ("dp", "seq")
    a, sent[-1]["out"] = lax.optimization_barrier((made[turns]["a"], sent[-1]["out"]))
    sum_a = lax.psum_scatter(a, axes, scatter_dimension=0, tiled=True)
    rest = branches(
        {"rest": rest_shape, "linear": ((length, taylor_cols), BF16)},
        [taylor_last, dense_second(1), window_second, dense_second(3)],
    )
    final = branches(
        {"gain": gain_shape, "returned": ((length, width), BF16)},
        [taylor_final] + [lambda s=s: {"gain": gains_of(s)} for s in (1, 2, 3)],
    )
    sum_a, rest["rest"] = lax.optimization_barrier((sum_a, rest["rest"]))
    sum_b, sum_c = unfolded(
        lax.psum_scatter(rest["rest"], axes, scatter_dimension=0, tiled=True)[0]
    )
    out_gain = lax.psum_scatter(final["gain"][0], axes, scatter_dimension=0, tiled=True)

    finals = [made[LAG * last + m]["final"] for m in range(CHUNKS)]
    block_out = spread(swapped(jnp.concatenate(finals, axis=0).reshape(2, block, width)), last)
    grad_tokens = spread(swapped(final["returned"].reshape(2, block, width)), 0)

    def narrow(value, used):
        return lambda: jnp.pad(value[:, :used].astype(F32), ((0, 0), (0, 2 * hidden_dim - used)))

    def dense_result():
        up_end = padded + hidden_dim - a_cols
        return jnp.concatenate(
            [sum_a[:, :hidden_dim], sum_a[:, padded:], sum_b[:, :up_end]], axis=1
        ).astype(F32)

    out_in = lax.switch(
        section,
        [narrow(sum_b, taylor_cols), dense_result, narrow(sum_a, window_cols), dense_result],
    )
    return (
        block_out,
        grad_tokens,
        out_in[None],
        sum_c.astype(F32)[None],
        out_gain[None],
    )


def solution(mesh):
    placed = (
        P("dp", "seq", None),
        P("section", None, None),
        P("section", None, None),
        P("section", None),
        P("dp", None),
        P("dp", "seq", None),
    )
    return jax.shard_map(
        local,
        mesh=mesh,
        in_specs=placed,
        out_specs=(
            P("dp", "seq", "section"),
            P("dp", "seq", "section"),
            P("section", ("dp", "seq"), None),
            P("section", ("dp", "seq"), None),
            P("section", ("dp", "seq")),
        ),
        check_vma=False,
    )
```

```python
import functools

import jax
import jax.numpy as jnp
from jax import lax
from jax.experimental import pallas as pl
from jax.experimental.pallas import tpu as pltpu
from jax.sharding import PartitionSpec as P

HEADS = 16
FEAT_DIM = 16
WINDOW = 64
CHUNKS = 4
LAG = 2
TILE = 256
PAIRS = HEADS // 2
epsilon = 1e-06

F32 = jnp.float32
BF16 = jnp.bfloat16


def nn(a, b):
    return jnp.dot(a, b, preferred_element_type=F32)


def nt(a, b):
    return lax.dot_general(a, b, (((1,), (1,)), ((), ())), preferred_element_type=F32)


def tn(a, b):
    return lax.dot_general(a, b, (((0,), (0,)), ((), ())), preferred_element_type=F32)


def lanes(rows, width):
    return lax.broadcasted_iota(jnp.int32, (rows, width), 1)


def call(kernel, grid, in_specs, out_specs, out_shape, scratch, flops):
    return pl.pallas_call(
        kernel,
        grid=grid,
        in_specs=in_specs,
        out_specs=out_specs,
        out_shape=out_shape,
        scratch_shapes=scratch,
        compiler_params=pltpu.CompilerParams(
            vmem_limit_bytes=40 * 1024 * 1024, dimension_semantics=("arbitrary",)
        ),
        cost_estimate=pl.CostEstimate(flops=flops, bytes_accessed=flops // 512, transcendentals=0),
    )


def whole(shape):
    return pl.BlockSpec(shape, lambda p: (0,) * len(shape))


def columns(rows, start=0, row=0):
    return pl.BlockSpec((rows, 128), lambda p: (row, start + p))


def finish(copies):
    for copy in copies:
        copy.wait()


IN_VMEM = pl.BlockSpec(memory_space=pltpu.VMEM)
IN_PLACE = pl.BlockSpec(memory_space=pl.ANY)


def plain_call(kernel, in_specs, out_specs, out_shape, scratch, flops):
    return pl.pallas_call(
        kernel,
        grid=(1,),
        in_specs=in_specs,
        out_specs=out_specs,
        out_shape=out_shape,
        scratch_shapes=scratch,
        compiler_params=pltpu.CompilerParams(vmem_limit_bytes=48 * 1024 * 1024),
        cost_estimate=pl.CostEstimate(flops=flops, bytes_accessed=flops // 512, transcendentals=0),
    )


def rms_inverse(inputs):
    return lax.rsqrt(jnp.mean(inputs * inputs, axis=-1, keepdims=True) + epsilon)


def rms_forward(inputs, gain_row):
    return (inputs * rms_inverse(inputs) * gain_row).astype(BF16)


def rms_backward(inputs, gain_row, grad_normed):
    inverse = rms_inverse(inputs)
    scaled = grad_normed * gain_row
    grad_inputs = inverse * scaled - inputs * inverse**3 * jnp.mean(
        scaled * inputs, axis=-1, keepdims=True
    )
    return grad_inputs


def pair_lanes(pair, start=0):
    return pl.ds(pl.multiple_of(start + pair * 128, 128), 128)


def stacked(value):
    lane = lanes(*value.shape)
    zero = jnp.zeros_like(value)
    return jnp.concatenate(
        [jnp.where(lane < 64, value, zero), jnp.where(lane < 64, zero, value)], axis=0
    )


def unstacked(value):
    rows = value.shape[0] // 2
    return jnp.where(lanes(rows, 128) < 64, value[:rows], value[rows:])


def twice(value, axis):
    return jnp.concatenate([value, value], axis=axis)


def taylor_mask(doc_t, doc_s, t_start, t_axis):
    t = t_start + lax.broadcasted_iota(jnp.int32, (doc_t == doc_s).shape, t_axis)
    s = lax.broadcasted_iota(jnp.int32, (doc_t == doc_s).shape, 1 - t_axis)
    return jnp.where((doc_t == doc_s) & (s <= t), 1.0, 0.0).astype(F32)


def taylor_queries(q, pair):
    wide = lanes(*q.shape) // FEAT_DIM
    zero = jnp.zeros_like(q)
    scaled = q * jnp.asarray(0.25, BF16)
    return jnp.concatenate(
        [jnp.where(wide == 2 * pair + i, scaled, zero) for i in range(2)], axis=0
    )


def taylor_forward_kernel(m, size, x_ref, gain_ref, docc, docr, in_ref, out_w_ref, *refs):
    earlier, refs = refs[:m], refs[m:]
    out_ref, kept_ref, mix_ref, den_ref, w_in, w_out, kv, mask, sems = refs
    rows = (m + 1) * size
    narrow, width = 2 * 128, x_ref.shape[1]
    cols = kept_ref.shape[1]
    reads = [
        pltpu.make_async_copy(
            in_ref.at[:, pl.ds(0, 2 * narrow)], w_in.at[:, pl.ds(0, 2 * narrow)], sems.at[0]
        ),
        pltpu.make_async_copy(
            in_ref.at[:, pl.ds(2 * narrow, width)], w_in.at[:, pl.ds(2 * narrow, width)], sems.at[1]
        ),
        pltpu.make_async_copy(out_w_ref.at[pl.ds(0, width), :], w_out, sems.at[2]),
    ] + [
        pltpu.make_async_copy(
            earlier[j].at[:, pl.ds(narrow, cols - narrow)],
            kv.at[pl.ds(j * size, size), :],
            sems.at[3 + j],
        )
        for j in range(m)
    ]
    for copy in reads:
        copy.start()
    inputs = x_ref[...].astype(F32)
    normed = rms_forward(inputs, gain_ref[...])
    mask[...] = taylor_mask(docc[m * size : rows, :], docr[:, :rows], m * size, 0)
    den_ref[...] = jnp.zeros_like(den_ref)
    reads[0].wait()
    kept_ref[:, : 2 * narrow] = nn(normed, w_in[:, : 2 * narrow]).astype(BF16)
    reads[1].wait()
    kept_ref[:, 2 * narrow :] = nn(normed, w_in[:, 2 * narrow :]).astype(BF16)
    kv[m * size : rows, :] = kept_ref[:, narrow:]
    finish(reads[3:])
    lane = lanes(size, 128)

    def one(pair, carry):
        a = nt(taylor_queries(kept_ref[:, :narrow], pair), kv[:, :narrow])
        w = (1.0 + a * (1.0 + 0.5 * a)) * twice(mask[...], 0)
        denom = jnp.sum(w, axis=1, keepdims=True)
        ratio = nn(w.astype(BF16), kv[:, pair_lanes(pair, narrow)]) / denom
        mix_ref[:, pair_lanes(pair)] = unstacked(ratio).astype(BF16)
        den_ref[...] = jnp.where(
            lane == 2 * pair,
            denom[:size],
            jnp.where(lane == 2 * pair + 1, denom[size:], den_ref[...]),
        )
        return carry

    lax.fori_loop(0, PAIRS, one, 0)
    reads[2].wait()
    out_ref[...] = (inputs + nn(mix_ref[...], w_out[...])).astype(BF16)


def taylor_forward(m, x, x_row, gain, docs, pack_in, pack_out, earlier):
    width = pack_in.shape[0]
    size = docs[0].shape[0] // CHUNKS
    cols = 2 * HEADS * FEAT_DIM + width
    low = jax.ShapeDtypeStruct((size, width), BF16)
    return plain_call(
        functools.partial(taylor_forward_kernel, m, size),
        [pl.BlockSpec((size, width), lambda p: (x_row, 0))] + [IN_VMEM] * 3 + [IN_PLACE] * (2 + m),
        [IN_VMEM] * 4,
        [
            low,
            jax.ShapeDtypeStruct((size, cols), BF16),
            low,
            jax.ShapeDtypeStruct((size, 128), F32),
        ],
        [
            pltpu.VMEM((width, cols), BF16),
            pltpu.VMEM((width, width), BF16),
            pltpu.VMEM(((m + 1) * size, cols - 256), BF16),
            pltpu.VMEM((size, (m + 1) * size), F32),
            pltpu.SemaphoreType.DMA((3 + m,)),
        ],
        2 * size * width * (cols + width),
    )(x, gain, *docs[:2], pack_in, pack_out, *earlier)


def taylor_backward_kernel(m, size, later, *refs):
    docc, docr, q_ref = refs[:3]
    refs = refs[3:]
    ks, vs = refs[: m + 1], refs[m + 1 : 2 * m + 2]
    dmix_ref, mix_ref, den_ref = refs[2 * m + 2 : 2 * m + 5]
    refs = refs[2 * m + 5 :]
    if later:
        dk_in, dv_in = refs[:2]
        refs = refs[2:]
    dq_ref, dk_ref, dv_ref, mask, k_all, k_turned, dq_turned = refs
    pair = pl.program_id(0)
    rows = (m + 1) * size

    @pl.when(pair == 0)
    def _():
        mask[...] = taylor_mask(docr[:, m * size : rows], docc[:rows, :], m * size, 1)
        for j in range(m + 1):
            k = ks[j][...]
            k_all[j * size : (j + 1) * size, :] = k
            k_turned[:, j * size : (j + 1) * size] = (k.astype(F32) * 0.25).T.astype(BF16)
        dk_ref[...] = jnp.zeros_like(dk_ref)
        if later:
            dk_ref[: m * size, :] = dk_in[...]

    lane = lanes(size, 128)
    dm = dmix_ref[...].astype(F32)
    both = dm * mix_ref[...].astype(F32)
    dnums, extras = [], []
    for i in range(2):
        inside = lane // 64 == i
        turn = 1.0 / jnp.sum(
            jnp.where(lane == 2 * pair + i, den_ref[...], 0.0), axis=1, keepdims=True
        )
        dden = -jnp.sum(jnp.where(inside, both, 0.0), axis=1, keepdims=True) * turn
        high = dden.astype(BF16).astype(F32)
        dnums.append(jnp.where(inside, dm * turn, 0.0).astype(BF16))
        extras.append(
            jnp.where(lane == 0, high, jnp.where(lane == 1, dden - high, 0.0)).astype(BF16)
        )
    dnum = jnp.concatenate(dnums, axis=0)
    dnum_more = jnp.concatenate([dnum, jnp.concatenate(extras, axis=0)], axis=1)
    q = taylor_queries(q_ref[...], pair)
    v = jnp.concatenate([part[...] for part in vs], axis=0)
    a = nt(k_all[...], q)
    masks = twice(mask[...], 1)
    w = (1.0 + a * (1.0 + 0.5 * a)) * masks
    dw = nt(jnp.concatenate([v, jnp.ones_like(v)], axis=1), dnum_more)
    da = (dw * (1.0 + a) * masks).astype(BF16)
    dv = nn(w.astype(BF16), dnum)
    if later:
        dv_ref[: m * size, :] = dv_in[...] + dv[: m * size]
        dv_ref[m * size :, :] = dv[m * size :]
    else:
        dv_ref[...] = dv
    dk_ref[...] += nn(da, q)
    own = pl.ds(pl.multiple_of(pair * 2 * FEAT_DIM, 2 * FEAT_DIM), 2 * FEAT_DIM)
    dq = nn(k_turned[own, :], da)
    dq_turned[own, :] = jnp.concatenate([dq[:FEAT_DIM, :size], dq[FEAT_DIM:, size:]], axis=0)

    @pl.when(pair == PAIRS - 1)
    def _():
        dq_ref[...] = dq_turned[...].T


def taylor_backward(m, docs, kept, dmix, mix, den, later):
    size = kept[0].shape[0]
    docc, docr = docs[:2]
    rows = (m + 1) * size
    return call(
        functools.partial(taylor_backward_kernel, m, size, later is not None),
        (PAIRS,),
        [whole(docc.shape), whole(docr.shape), whole((size, 256))]
        + [pl.BlockSpec((size, 256), lambda p: (0, 1))] * (m + 1)
        + [columns(size, 4)] * (m + 1)
        + [columns(size), columns(size), whole((size, 128))]
        + ([whole((m * size, 256)), columns(m * size)] if later is not None else []),
        [whole((size, 256)), whole((rows, 256)), columns(rows)],
        [
            jax.ShapeDtypeStruct((size, 256), F32),
            jax.ShapeDtypeStruct((rows, 256), F32),
            jax.ShapeDtypeStruct((rows, HEADS * 64), F32),
        ],
        [
            pltpu.VMEM((rows, size), F32),
            pltpu.VMEM((rows, 256), BF16),
            pltpu.VMEM((256, rows), BF16),
            pltpu.VMEM((256, size), F32),
        ],
        5 * HEADS * (m + 1) * size * size * 512,
    )(docc, docr, kept[m], *kept, *kept, dmix, mix, den, *(later or ()))


STEP = 128
UNROLL = 4


def window_docs(docs):
    return jnp.concatenate([jnp.full((STEP,), -1, jnp.int32), docs])[:, None]


def window_biases(m, size, docc, docr, bias):
    s = lax.broadcasted_iota(jnp.int32, (2 * STEP, STEP), 0)
    t = STEP + lax.broadcasted_iota(jnp.int32, (2 * STEP, STEP), 1)
    near = (t >= s) & (t - s < WINDOW)
    for b in range(size // STEP):
        at = m * size + b * STEP
        same = docr[:, at : at + STEP] == docc[at : at + 2 * STEP, :]
        bias[b] = jnp.where(near & same, 0.0, -1e30).astype(F32)


def window_weights(k, q, bias):
    a = nt(k, q) + twice(bias, 1)
    p = jnp.exp(a - jnp.max(a, axis=0, keepdims=True))
    return p * (1.0 / jnp.sum(p, axis=0, keepdims=True))


def joined(before, own, cut):
    value = own[:, cut]
    first = before[:, cut] if before is not None else jnp.zeros((STEP, 128), BF16)
    return jnp.concatenate([first, value], axis=0)


def window_forward_kernel(m, size, x_ref, gain_ref, docc, docr, in_ref, out_w_ref, *refs):
    before, refs = (refs[0], refs[1:]) if m > 0 else (None, refs)
    out_ref, kept_ref, mix_ref, w_in, w_out, bias, sems = refs
    width = x_ref.shape[1]
    reads = [
        pltpu.make_async_copy(
            in_ref.at[:, pl.ds(i * width, width)], w_in.at[:, pl.ds(i * width, width)], sems.at[i]
        )
        for i in range(3)
    ] + [pltpu.make_async_copy(out_w_ref.at[pl.ds(0, width), :], w_out, sems.at[3])]
    for copy in reads:
        copy.start()
    inputs = x_ref[...].astype(F32)
    normed = rms_forward(inputs, gain_ref[...])
    for i in range(3):
        cut = slice(i * width, (i + 1) * width)
        reads[i].wait()
        kept_ref[:, cut] = nn(normed, w_in[:, cut]).astype(BF16)

    window_biases(m, size, docc, docr, bias)

    def one(pair, carry):
        cuts = [pair_lanes(pair, i * width) for i in range(3)]
        k_all = joined(before, kept_ref, cuts[1])
        v_all = joined(before, kept_ref, cuts[2])
        for b in range(size // STEP):
            own = slice(b * STEP, (b + 1) * STEP)
            keys = slice(b * STEP, (b + 2) * STEP)
            q = stacked(kept_ref[own, cuts[0]] * jnp.asarray(0.125, BF16))
            p = window_weights(k_all[keys], q, bias[b])
            mix_ref[own, cuts[0]] = unstacked(tn(p.astype(BF16), v_all[keys])).astype(BF16)
        return carry

    lax.fori_loop(0, PAIRS, one, 0, unroll=UNROLL)
    reads[3].wait()
    out_ref[...] = (inputs + nn(mix_ref[...], w_out[...])).astype(BF16)


def before_spec(size, cols):
    return pl.BlockSpec((STEP, cols), lambda p: (size // STEP - 1, 0))


def window_forward(m, x, gain, docs, pack_in, pack_out, before):
    size, width = x.shape
    low = jax.ShapeDtypeStruct((size, width), BF16)
    more = [before_spec(size, 3 * width)] if m > 0 else []
    return plain_call(
        functools.partial(window_forward_kernel, m, size),
        [IN_VMEM] * 4 + [IN_PLACE] * 2 + more,
        [IN_VMEM] * 3,
        [low, jax.ShapeDtypeStruct((size, 3 * width), BF16), low],
        [
            pltpu.VMEM((width, 3 * width), BF16),
            pltpu.VMEM((width, width), BF16),
            pltpu.VMEM((size // STEP, 2 * STEP, STEP), F32),
            pltpu.SemaphoreType.DMA((4,)),
        ],
        8 * size * width * width,
    )(x, gain, docs[2], docs[1], pack_in, pack_out, *([before] if m > 0 else []))


def window_backward_kernel(m, size, docc, docr, kept_ref, g_ref, out_w_ref, *refs):
    w_out, dmix, bias, sems = refs[-4:]
    refs = refs[:-4]
    before = None
    if m > 0:
        before, part_ref, x_ref, gain_ref, g_before_ref, in_ref = refs[:6]
        grad_ref, out_ref, done_ref, w_in = refs[6:]
    else:
        (grad_ref,) = refs
    width = g_ref.shape[1]
    first = pltpu.make_async_copy(out_w_ref.at[pl.ds(0, width), :], w_out, sems.at[3])
    first.start()
    reads = []
    if m > 0:
        reads = [
            pltpu.make_async_copy(
                in_ref.at[:, pl.ds(i * width, width)],
                w_in.at[:, pl.ds(i * width, width)],
                sems.at[i],
            )
            for i in range(3)
        ]
        for copy in reads:
            copy.start()
        done_ref[...] = part_ref[...]
    first.wait()
    dmix[...] = nt(g_ref[...], w_out[...]).astype(BF16)

    window_biases(m, size, docc, docr, bias)

    def one(pair, carry):
        cuts = [pair_lanes(pair, i * width) for i in range(3)]
        k_all = joined(before, kept_ref, cuts[1])
        v_all = joined(before, kept_ref, cuts[2])
        blocks = size // STEP
        halves = [[0.0] * (blocks + 1) for _ in range(2)]
        for b in range(blocks):
            own = slice(b * STEP, (b + 1) * STEP)
            keys = slice(b * STEP, (b + 2) * STEP)
            q = stacked(kept_ref[own, cuts[0]] * jnp.asarray(0.125, BF16))
            dm = stacked(dmix[own, cuts[0]])
            k, v = k_all[keys], v_all[keys]
            p = window_weights(k, q, bias[b])
            dp = nt(v, dm)
            da = (p * (dp - jnp.sum(p * dp, axis=0, keepdims=True))).astype(BF16)
            for half, more in zip(halves, (nn(da, q), nn(p.astype(BF16), dm))):
                half[b] = half[b] + more[:STEP]
                half[b + 1] = more[STEP:]
            dq = unstacked(tn(da, k * jnp.asarray(0.125, BF16)))
            grad_ref[own, cuts[0]] = dq.astype(BF16)
        for half, cut in zip(halves, cuts[1:]):
            grad_ref[:, cut] = jnp.concatenate(half[1:], axis=0).astype(BF16)
            if m > 0:
                tail = slice(size - STEP, size)
                done_ref[tail, cut] = (part_ref[tail, cut].astype(F32) + half[0]).astype(BF16)
        return carry

    lax.fori_loop(0, PAIRS, one, 0, unroll=UNROLL)
    if m > 0:
        total = 0.0
        for i in range(3):
            cut = slice(i * width, (i + 1) * width)
            reads[i].wait()
            total = total + nt(done_ref[:, cut], w_in[:, cut])
        grad = rms_backward(x_ref[...].astype(F32), gain_ref[...], total)
        out_ref[...] = (g_before_ref[...].astype(F32) + grad).astype(BF16)


def window_backward(m, docs, kept, g, pack_out, before, settle):
    size, width = g.shape
    low = jax.ShapeDtypeStruct((size, width), BF16)
    wide = jax.ShapeDtypeStruct((size, 3 * width), BF16)
    more, arrays = [], []
    if m > 0:
        more = [before_spec(size, 3 * width)] + [IN_VMEM] * 4 + [IN_PLACE]
        arrays = [before, *settle]
    return plain_call(
        functools.partial(window_backward_kernel, m, size),
        [IN_VMEM] * 4 + [IN_PLACE] + more,
        [IN_VMEM] * (3 if m > 0 else 1),
        [wide] + ([low, wide] if m > 0 else []),
        ([pltpu.VMEM((width, 3 * width), BF16)] if m > 0 else [])
        + [
            pltpu.VMEM((width, width), BF16),
            pltpu.VMEM((size, width), BF16),
            pltpu.VMEM((size // STEP, 2 * STEP, STEP), F32),
            pltpu.SemaphoreType.DMA((4,)),
        ],
        16 * size * width * width,
    )(docs[2], docs[1], kept, g, pack_out, *arrays)


def blank(shapes):
    return pl.pallas_call(
        lambda *refs: None,
        out_specs=[pl.BlockSpec(memory_space=pl.ANY)] * len(shapes),
        out_shape=[jax.ShapeDtypeStruct(*shape) for shape in shapes],
    )()


def spans(width):
    return (2, width // 2) if width % 256 == 0 else (1, width)


def tile_copies(refs, sems, n, w):
    made = []
    for i, (a, b, start) in enumerate(refs):
        cut = pl.ds(pl.multiple_of(start + n * w, 128), w)
        made.append(pltpu.make_async_copy(a.at[:, cut], b.at[:, cut], sems.at[n, i]))
    return made


def start_all(refs, sems, count, w):
    for n in range(count):
        for copy in tile_copies(refs, sems, n, w):
            copy.start()


def out_copies(wo_ref, wo, sems, count, w):
    rows = wo_ref.shape[0]
    if wo.shape[0] > rows:
        wo[rows:, :] = jnp.zeros((wo.shape[0] - rows, wo.shape[1]), BF16)
    made = []
    for n in range(count):
        cut = pl.ds(n * w, min(w, rows - n * w))
        made.append(pltpu.make_async_copy(wo_ref.at[cut, :], wo.at[cut, :], sems.at[n]))
    return made


def wait_for(copies, n):
    for i, copy in enumerate(copies):
        pl.when(n == i)(copy.wait)


def dense_forward_kernel(
    x_ref,
    gain_ref,
    wg_ref,
    wu_ref,
    wo_ref,
    out_ref,
    gate_ref,
    up_ref,
    wg,
    wu,
    wo,
    gates,
    ups,
    normed,
    total,
    sems,
    out_sems,
    done,
):
    count, w = spans(gates.shape[1])
    reads = [(wg_ref, wg, 0), (wu_ref, wu, 0)]
    writes = [(gates, gate_ref, 0), (ups, up_ref, 0)]
    start_all(reads, sems, count, w)
    outs = out_copies(wo_ref, wo, out_sems, count, w)
    for copy in outs:
        copy.start()
    inputs = x_ref[...].astype(F32)
    normed[...] = rms_forward(inputs, gain_ref[...])
    total[...] = inputs

    def tile(n, carry):
        cut = pl.ds(pl.multiple_of(n * w, 128), w)
        came = tile_copies(reads, sems, n, w)
        came[0].wait()
        gate = nn(normed[...], wg[:, cut])
        came[1].wait()
        up = nn(normed[...], wu[:, cut])
        gates[:, cut] = gate.astype(BF16)
        ups[:, cut] = up.astype(BF16)
        for copy in tile_copies(writes, done, n, w):
            copy.start()
        hidden = (gate * jax.nn.sigmoid(gate) * up).astype(BF16)
        wait_for(outs, n)
        total[...] += nn(hidden, wo[cut, :])
        return carry

    lax.fori_loop(0, count, tile, 0)
    out_ref[...] = total[...].astype(BF16)
    for n in range(count):
        finish(tile_copies(writes, done, n, w))


def weight_scratch(width, padded):
    return [pltpu.VMEM((width, padded), BF16)] * 2 + [pltpu.VMEM((padded, width), BF16)]


def dense_forward(x, gain, weights):
    size, width = x.shape
    padded = weights[1].shape[1]
    tiles = spans(padded)[0]
    return plain_call(
        dense_forward_kernel,
        [IN_VMEM, IN_VMEM] + [IN_PLACE] * 3,
        [IN_VMEM, IN_PLACE, IN_PLACE],
        [jax.ShapeDtypeStruct((size, width), BF16)]
        + [jax.ShapeDtypeStruct((size, padded), BF16)] * 2,
        weight_scratch(width, padded)
        + [pltpu.VMEM((size, padded), BF16)] * 2
        + [pltpu.VMEM((size, width), BF16), pltpu.VMEM((size, width), F32)]
        + [pltpu.SemaphoreType.DMA(shape) for shape in ((tiles, 2), (tiles,), (tiles, 2))],
        6 * size * width * padded,
    )(x, gain, *weights)


def dense_backward_kernel(
    x_ref,
    gain_ref,
    g_ref,
    gate_ref,
    up_ref,
    wg_ref,
    wu_ref,
    wo_ref,
    out_ref,
    grad_ref,
    hidden_ref,
    wg,
    wu,
    wo,
    gates,
    ups,
    grads,
    hiddens,
    total,
    sems,
    out_sems,
    done,
):
    count, w = spans(gates.shape[1])
    reads = [(gate_ref, gates, 0), (up_ref, ups, 0), (wg_ref, wg, 0), (wu_ref, wu, 0)]
    writes = [(hiddens, hidden_ref, 0), (grads, grad_ref, 0), (grads, grad_ref, count * w)]
    outs = out_copies(wo_ref, wo, out_sems, count, w)
    for copy in outs:
        copy.start()
    start_all(reads, sems, count, w)
    total[...] = jnp.zeros_like(total)

    def tile(n, carry):
        cut = pl.ds(pl.multiple_of(n * w, 128), w)
        came = tile_copies(reads, sems, n, w)
        wait_for(outs, n)
        finish(came[:2])
        dh = nt(g_ref[...], wo[cut, :])
        gate = gates[:, cut].astype(F32)
        up = ups[:, cut].astype(F32)
        sg = jax.nn.sigmoid(gate)
        active = gate * sg
        hiddens[:, cut] = (active * up).astype(BF16)
        dgate = (dh * up * (sg + active * (1.0 - sg))).astype(BF16)
        dup = (dh * active).astype(BF16)
        grads[:, cut] = dgate
        grads[:, pl.ds(pl.multiple_of((count + n) * w, 128), w)] = dup
        for copy in tile_copies(writes, done, n, w):
            copy.start()
        finish(came[2:])
        total[...] += nt(dgate, wg[:, cut]) + nt(dup, wu[:, cut])
        return carry

    lax.fori_loop(0, count, tile, 0)
    grad = rms_backward(x_ref[...].astype(F32), gain_ref[...], total[...])
    out_ref[...] = (g_ref[...].astype(F32) + grad).astype(BF16)
    for n in range(count):
        finish(tile_copies(writes, done, n, w))


def dense_backward(x, gain, g, gate, up, weights):
    size, width = x.shape
    padded = weights[1].shape[1]
    tiles = spans(padded)[0]
    return plain_call(
        dense_backward_kernel,
        [IN_VMEM] * 3 + [IN_PLACE] * 5,
        [IN_VMEM] + [IN_PLACE] * 2,
        [jax.ShapeDtypeStruct((size, w), BF16) for w in (width, 2 * padded, padded)],
        weight_scratch(width, padded)
        + [pltpu.VMEM((size, w), BF16) for w in (padded, padded, 2 * padded, padded)]
        + [pltpu.VMEM((size, width), F32)]
        + [pltpu.SemaphoreType.DMA(shape) for shape in ((tiles, 4), (tiles,), (tiles, 3))],
        6 * size * width * padded,
    )(x, gain, g, gate, up, *weights)


def dense_both_kernel(
    x_ref,
    gain_ref,
    g_ref,
    wg_ref,
    wu_ref,
    wo_ref,
    out_ref,
    grad_ref,
    hidden_ref,
    wg,
    wu,
    wo,
    grads,
    hiddens,
    normed,
    total,
    sems,
    out_sems,
    done,
):
    count, w = spans(hiddens.shape[1])
    reads = [(wg_ref, wg, 0), (wu_ref, wu, 0)]
    writes = [(hiddens, hidden_ref, 0), (grads, grad_ref, 0), (grads, grad_ref, count * w)]
    start_all(reads, sems, count, w)
    outs = out_copies(wo_ref, wo, out_sems, count, w)
    for copy in outs:
        copy.start()
    inputs = x_ref[...].astype(F32)
    normed[...] = rms_forward(inputs, gain_ref[...])
    total[...] = jnp.zeros_like(total)

    def tile(n, carry):
        cut = pl.ds(pl.multiple_of(n * w, 128), w)
        came = tile_copies(reads, sems, n, w)
        came[0].wait()
        gate = nn(normed[...], wg[:, cut])
        came[1].wait()
        up = nn(normed[...], wu[:, cut])
        sg = jax.nn.sigmoid(gate)
        active = gate * sg
        hiddens[:, cut] = (active * up).astype(BF16)
        wait_for(outs, n)
        dh = nt(g_ref[...], wo[cut, :])
        dgate = (dh * up * (sg + active * (1.0 - sg))).astype(BF16)
        dup = (dh * active).astype(BF16)
        grads[:, cut] = dgate
        grads[:, pl.ds(pl.multiple_of((count + n) * w, 128), w)] = dup
        for copy in tile_copies(writes, done, n, w):
            copy.start()
        total[...] += nt(dgate, wg[:, cut]) + nt(dup, wu[:, cut])
        return carry

    lax.fori_loop(0, count, tile, 0)
    grad = rms_backward(inputs, gain_ref[...], total[...])
    out_ref[...] = (g_ref[...].astype(F32) + grad).astype(BF16)
    for n in range(count):
        finish(tile_copies(writes, done, n, w))


def dense_both(x, gain, g, weights):
    size, width = x.shape
    padded = weights[1].shape[1]
    tiles = spans(padded)[0]
    return plain_call(
        dense_both_kernel,
        [IN_VMEM] * 3 + [IN_PLACE] * 3,
        [IN_VMEM] + [IN_PLACE] * 2,
        [jax.ShapeDtypeStruct((size, w), BF16) for w in (width, 2 * padded, padded)],
        weight_scratch(width, padded)
        + [pltpu.VMEM((size, w), BF16) for w in (2 * padded, padded)]
        + [pltpu.VMEM((size, width), BF16)]
        + [pltpu.VMEM((size, width), F32)]
        + [pltpu.SemaphoreType.DMA(shape) for shape in ((tiles, 2), (tiles,), (tiles, 3))],
        10 * size * width * padded,
    )(x, gain, g, *weights)


def turn_kernel(x_ref, gain_ref, out_ref):
    normed = rms_forward(x_ref[...].astype(F32), gain_ref[...])
    out_ref[...] = normed.astype(F32).T.astype(BF16)


def turned_norm(gain, x):
    rows, width = x.shape
    return call(
        turn_kernel,
        (rows // TILE,),
        [pl.BlockSpec((TILE, width), lambda j: (j, 0)), whole((1, width))],
        pl.BlockSpec((width, TILE), lambda j: (0, j)),
        jax.ShapeDtypeStruct((width, rows), BF16),
        [],
        8 * rows * width,
    )(x, gain)


def grad_in_kernel(count, tiles, turned_ref, *refs):
    groups = [refs[count * n : count * (n + 1)] for n in range(len(tiles))]
    out_ref, joined_ref = refs[count * len(tiles) :]
    step = pl.program_id(0)
    size = joined_ref.shape[0] // count
    start = 0
    for parts, (_, used) in zip(groups, tiles):

        @pl.when((step >= start) & (step < start + used))
        def _(parts=parts):
            for c, part in enumerate(parts):
                joined_ref[c * size : (c + 1) * size, :] = part[...]

        start += used

    def rows(i, carry):
        cut = pl.ds(pl.multiple_of(i * 2 * TILE, 2 * TILE), 2 * TILE)
        out_ref[cut, :] = nn(turned_ref[cut, :], joined_ref[...]).astype(BF16)
        return carry

    lax.fori_loop(0, turned_ref.shape[0] // (2 * TILE), rows, 0)


def grad_in(turned, groups, out_width, tile):
    width, length = turned.shape
    count = len(groups[0][0])
    size = length // count
    specs = [whole((width, length))]
    arrays, begun = [], 0
    for parts, first, used in groups:

        def at(j, first=first, used=used, begun=begun):
            return (0, first + jnp.clip(j - begun, 0, used - 1))

        specs += [pl.BlockSpec((size, tile), at)] * count
        arrays += parts
        begun += used
    return call(
        functools.partial(grad_in_kernel, count, [group[1:] for group in groups]),
        (begun,),
        specs,
        pl.BlockSpec((width, tile), lambda j: (0, j)),
        jax.ShapeDtypeStruct((width, out_width), BF16),
        [pltpu.VMEM((length, tile), BF16)],
        2 * length * width * tile * begun,
    )(turned, *arrays)


def grad_out_kernel(count, used, *refs):
    left, right = refs[:count], refs[count : 2 * count]
    out_ref = refs[2 * count]
    step = pl.program_id(0)

    @pl.when(step < used)
    def _():
        joined = jnp.concatenate([part[...] for part in left], axis=0)
        turned = joined.astype(F32).T.astype(BF16)
        out_ref[...] = nn(turned, jnp.concatenate([part[...] for part in right], axis=0)).astype(
            BF16
        )

    @pl.when(step >= used)
    def _():
        out_ref[...] = jnp.zeros_like(out_ref)


def grad_out(left, right, used, rows):
    count = len(left)
    size, width = right[0].shape
    tiles = -(-rows // TILE)
    return call(
        functools.partial(grad_out_kernel, count, used),
        (tiles,),
        [pl.BlockSpec((size, TILE), lambda j: (0, jnp.minimum(j, used - 1)))] * count
        + [whole((size, width))] * count,
        pl.BlockSpec((TILE, width), lambda j: (j, 0)),
        jax.ShapeDtypeStruct((rows, width), BF16),
        [],
        2 * count * size * width * TILE * used,
    )(*left, *right)


def result_kernel(
    hidden, gates, fold, a_used, b_used, where_ref, a_ref, rest_ref, gain_ref, in_ref, *refs
):
    out_in_ref, out_out_ref, out_gain_ref, rows, sem = refs
    section = where_ref[0]
    copy = pltpu.make_async_copy(
        in_ref.at[pl.ds(pl.multiple_of(where_ref[1] * fold, fold), fold), :], rows, sem
    )
    copy.start()
    rest = rest_ref[...].astype(F32)
    width = rest.shape[1]
    below = rest.shape[0] - out_out_ref.shape[0]
    out_out_ref[...] = rest[below:]
    step = below - fold
    extra = width * step // fold
    right = jnp.concatenate(
        [rest[fold:below, i * extra : (i + 1) * extra] for i in range(width // extra)], axis=0
    )
    b = jnp.concatenate([rest[:fold], right], axis=1)

    @pl.when(section % 2 == 1)
    def _():
        a = a_ref[...].astype(F32)
        up = jnp.concatenate([a[:, gates:], b], axis=1)
        first = hidden // 128 * 128
        turned = pltpu.roll(up, hidden - first, 1)
        out_in_ref[:, :first] = a[:, :first]
        out_in_ref[:, first : first + 128] = jnp.where(
            lanes(fold, 128) < hidden - first, a[:, first : first + 128], turned[:, :128]
        )
        out_in_ref[:, first + 128 :] = turned[:, 128 : 2 * hidden - first]

    @pl.when(section % 2 == 0)
    def _():
        out_in_ref[...] = jnp.zeros_like(out_in_ref)

    @pl.when(section == 0)
    def _():
        out_in_ref[:, :b_used] = b[:, :b_used]

    @pl.when(section == 2)
    def _():
        out_in_ref[:, :a_used] = a_ref[:, :a_used].astype(F32)

    copy.wait()
    total = jnp.sum(rows[...].astype(F32) * out_in_ref[...], axis=1, keepdims=True)
    out_gain_ref[...] = total / gain_ref[...]


def result(where, a, rest, gain, pack_in, hidden, gates, owners, a_used, b_used):
    width, cols = pack_in.shape
    fold = width // owners
    return plain_call(
        functools.partial(result_kernel, hidden, gates, fold, a_used, b_used),
        [pl.BlockSpec(memory_space=pltpu.SMEM)] + [IN_VMEM] * 3 + [IN_PLACE],
        [IN_VMEM] * 3,
        [
            jax.ShapeDtypeStruct((fold, cols), F32),
            jax.ShapeDtypeStruct((hidden // owners, width), F32),
            jax.ShapeDtypeStruct((fold, 1), F32),
        ],
        [pltpu.VMEM((fold, cols), BF16), pltpu.SemaphoreType.DMA(())],
        2 * fold * cols,
    )(where, a, rest, gain, pack_in)


def local(tokens, section_in, section_out, gains, bounds, cotangent):
    section = lax.axis_index("section")
    seq = lax.axis_index("seq")
    sections = lax.axis_size("section")
    pack_in = section_in[0]
    pack_out = section_out[0]
    gain_row = gains
    _, block, width = tokens.shape
    hidden_dim = pack_out.shape[0]
    padded = -(-hidden_dim // TILE) * TILE
    length = 2 * block
    size = length // CHUNKS
    taylor_cols = 2 * HEADS * FEAT_DIM + width
    window_cols = 3 * width
    last = sections - 1

    def swapped(two):
        away = lax.dynamic_index_in_dim(two, 1 - seq, 0, keepdims=False)
        own = lax.dynamic_index_in_dim(two, seq, 0, keepdims=False)
        came = lax.ppermute(away, "seq", [(0, 1), (1, 0)])
        return jnp.where(seq == 0, jnp.stack([own, came]), jnp.stack([came, own]))

    def branches(shapes, makers):
        names = list(shapes)

        def branch(maker):
            def run():
                made = maker() if maker is not None else {}
                missing = [name for name in names if name not in made]
                empty = dict(zip(missing, blank([shapes[name] for name in missing]))) if missing else {}
                return tuple(made[name] if name in made else empty[name] for name in names)

            return run

        order = (2,3,1,0)
        place = sum(jnp.where(section == s, i, 0) for i, s in enumerate(order))
        values = lax.switch(place, [branch(makers[s]) for s in order])
        return dict(zip(names, values))

    starts = lax.dynamic_index_in_dim(bounds, seq, 0, keepdims=False)
    positions = jnp.arange(length, dtype=jnp.int32)
    docs = jnp.sum((starts[None, :] <= positions[:, None]).astype(jnp.int32), axis=1)
    docs = (docs[:, None], docs[None, :], window_docs(docs))

    feed = swapped(tokens).reshape(length, width)
    wanted = swapped(cotangent).reshape(length, width)

    def fed(m):
        return feed[m * size : (m + 1) * size]

    first_back = (last + 1) * LAG
    turns = first_back + LAG + CHUNKS + 1
    low = ((size, width), BF16)
    wide = ((size, padded), BF16)
    made, sent = [], []

    def prepare():
        up = pack_in[:, hidden_dim:]
        return {"wu": jnp.pad(up, ((0, 0), (0, padded - hidden_dim)))}

    def prepare_more():
        more = padded - hidden_dim
        return {
            "wg": jnp.pad(pack_in[:, :hidden_dim], ((0, 0), (0, more))),
            "wo": jnp.pad(pack_out, ((0, more), (0, 0))),
        }

    def entry(s, m):
        return fed(m) if s == 0 else sent[m + LAG * (s - 1)]["out"]

    def upstream(s, m):
        if s == last:
            return wanted[m * size : (m + 1) * size]
        if s == 2:
            return sent[m + LAG * last]["out"]
        return sent[first_back + 1 + LAG * (1 - s) + m]["out"]

    def taylor_turn(m):
        def run():
            earlier = [made[i]["linear"] for i in range(m)]
            out, projected, mix, den = taylor_forward(
                m, feed, m, gain_row, docs, pack_in, pack_out, earlier
            )
            return {"out": out, "linear": projected, "mix": mix, "den": den}

        return run

    def dense_turn(m):
        def run():
            out, gate, up = dense_forward(entry(1, m), gain_row, weights)
            return {"out": out, "gate": gate, "up": up}

        return run

    def window_turn(m):
        def run():
            before = made[2 * LAG + m - 1]["window"] if m > 0 else None
            out, projected, mix = window_forward(
                m, entry(2, m), gain_row, docs, pack_in, pack_out, before
            )
            return {"out": out, "window": projected, "mix": mix}

        return run

    def dense_both_turn(m):
        def run():
            out, grad, hidden = dense_both(entry(3, m), gain_row, upstream(3, m), weights)
            return {"out": out, "grad": grad, "hidden": hidden}

        return run

    def dense_final():
        blocks = range(CHUNKS)
        inputs = jnp.concatenate([entry(last, m) for m in blocks], axis=0).astype(F32)
        hidden = jnp.concatenate([made[LAG * last + m]["hidden"] for m in blocks], axis=0)
        return {"final": (inputs + nn(hidden, weights[2])).astype(BF16)}

    def turned(s):
        def run():
            x = jnp.concatenate([entry(s, m) for m in range(CHUNKS)], axis=0) if s else feed
            return {"turned": turned_norm(gain_row, x)}

        return run

    turned_at = {0: first_back, 1: first_back, 3: first_back + 3, 2: turns - 1}

    def turned_of(s):
        return made[turned_at[s]]["turned"]

    def window_back(m):
        def run():
            if m == CHUNKS:
                done = made[first_back + m - 1]["part"]
                grad = rms_backward(
                    entry(2, m - 1).astype(F32), gain_row, nt(done, pack_in[:, :window_cols])
                )
                out = (upstream(2, m - 1).astype(F32) + grad).astype(BF16)
                return {"out": out, "done": done}
            before = made[2 * LAG + m - 1]["window"] if m > 0 else None
            settle = ()
            if m > 0:
                settle = (
                    made[first_back + m - 1]["part"],
                    entry(2, m - 1),
                    gain_row,
                    upstream(2, m - 1),
                    pack_in,
                )
            results = window_backward(
                m, docs, made[2 * LAG + m]["window"], upstream(2, m), pack_out, before, settle
            )
            values = {"part": results[0]}
            if m > 0:
                values.update(out=results[1], done=results[2])
            return values

        return run

    def dense_back(m):
        def run():
            kept = made[LAG + m]
            out, grad, hidden = dense_backward(
                entry(1, m), gain_row, upstream(1, m), kept["gate"], kept["up"], weights
            )
            return {"out": out, "grad": grad, "hidden": hidden}

        return run

    def taylor_back(ms, earlier):
        dqs = []
        for m in ms:
            dmix = nt(upstream(0, m), pack_out[:width]).astype(BF16)
            dq, dk, dv = taylor_backward(
                m,
                docs,
                [made[i]["linear"] for i in range(m + 1)],
                dmix,
                made[m]["mix"],
                made[m]["den"],
                earlier,
            )
            earlier = (dk, dv)
            dqs.append(dq)
        return dqs, earlier

    def taylor_turn_back(m):
        def run():
            earlier = (made[-1]["dk"], made[-1]["dv"]) if m > 0 else None
            dqs, (dk, dv) = taylor_back([m], earlier)
            return {"dq": dqs[0], "dk": dk, "dv": dv}

        return run

    def spread(two, source):
        share = width // sections
        mine = two[:, :, source * share : (source + 1) * share]
        for target in range(sections):
            if target != source:
                piece = two[:, :, target * share : (target + 1) * share]
                came = lax.ppermute(piece, "section", [(source, target)])
                mine = jnp.where(section == target, came, mine)
        return mine

    taylor_shapes = {}
    for t in range(turns + 1):
        shapes, makers, pairs = {}, [None] * sections, []
        for s in range(sections):
            m = t - LAG * s
            if 0 <= m < CHUNKS:
                shapes["out"] = low
                makers[s] = (taylor_turn, dense_turn, window_turn, dense_both_turn)[s](m)
                if s == 0:
                    shapes.update(linear=((size, taylor_cols), BF16), mix=low)
                    shapes["den"] = ((size, 128), F32)
                elif s == 1:
                    shapes.update(gate=wide, up=wide)
                elif s == 2:
                    shapes.update(window=((size, window_cols), BF16), mix=low)
                else:
                    shapes.update(grad=((size, 2 * padded), BF16), hidden=wide)
                pairs.append((s, s + 1) if s < last else (s, s - 1))
        if t == 0:
            shapes["wu"] = ((width, padded), BF16)
            makers[1] = makers[3] = prepare
        if t == 1:
            shapes.update(wg=((width, padded), BF16), wo=((padded, width), BF16))
            makers[1] = makers[3] = prepare_more
        m = t - first_back
        if 0 <= m <= CHUNKS:
            makers[2] = window_back(m)
            if m < CHUNKS:
                shapes["part"] = ((size, window_cols), BF16)
            if m > 0:
                shapes.update(out=low, done=((size, window_cols), BF16))
                pairs.append((2, 1))
        m = t - first_back - 1 - LAG
        if 0 <= m < CHUNKS:
            makers[1] = dense_back(m)
            shapes.update(out=low, grad=((size, 2 * padded), BF16), hidden=wide)
            pairs.append((1, 0))
        m = t - first_back - 1 - 2 * LAG
        if 0 <= m < CHUNKS - 1:
            makers[0] = taylor_turn_back(m)
            rows = (m + 1) * size
            taylor_shapes = {
                "dq": ((size, 256), F32),
                "dk": ((rows, 256), F32),
                "dv": ((rows, width), F32),
            }
            shapes.update(taylor_shapes)
        for s, at in turned_at.items():
            if t == at:
                makers[s] = turned(s)
                shapes["turned"] = ((width, length), BF16)
        if t == turns:
            break
        made.append(branches(shapes, makers))
        if t == 1:
            weights = (made[1]["wg"], made[0]["wu"], made[1]["wo"])
        sent.append({"out": lax.ppermute(made[t]["out"], "section", pairs)} if pairs else {})

    def turns_of(s):
        start = (0, first_back + 1 + LAG, first_back + 1, LAG * last)[s]
        return made[start : start + CHUNKS]

    def every(s, name):
        return [value[name] for value in turns_of(s)]

    def entries(s):
        return [entry(s, m) for m in range(CHUNKS)]

    def upstreams(s):
        return [upstream(s, m) for m in range(CHUNKS)]

    tile = 2 * TILE
    b_cols = taylor_cols
    owners = lax.axis_size("dp") * lax.axis_size("seq")
    a_cols = 2 * padded - b_cols
    a_shape = ((width, a_cols), BF16)
    fold = width // owners
    rest_rows = fold * b_cols // width + hidden_dim // owners
    rest_shape = ((owners, rest_rows, width), BF16)

    def folded(b, c):
        b = b.reshape(owners, fold, b_cols)
        parts = [b[:, :, :width]]
        extra = b_cols - width
        count = width // extra
        step = fold // count
        parts.append(
            jnp.concatenate(
                [b[:, i * step : (i + 1) * step, width:] for i in range(count)], axis=2
            )
        )
        return {"rest": jnp.concatenate(parts + [c.reshape(owners, -1, width)], axis=1)}

    def dense_first(s):
        def run():
            groups = [(every(s, "grad"), 0, a_cols // tile)]
            return {"a": grad_in(turned_of(s), groups, a_cols, tile)}

        return run

    def window_first():
        groups = [(every(2, "done"), 0, window_cols // tile)]
        return {"a": grad_in(turned_of(2), groups, a_cols, tile)}

    def dense_second(s):
        def run():
            groups = [(every(s, "grad"), a_cols // tile, b_cols // tile)]
            return folded(
                grad_in(turned_of(s), groups, b_cols, tile),
                grad_out(every(s, "hidden"), upstreams(s), padded // TILE, hidden_dim),
            )

        return run

    def window_second():
        mixes = [made[2 * LAG + m]["mix"] for m in range(CHUNKS)]
        (unused,) = blank([((width, b_cols), BF16)])
        return folded(unused, grad_out(mixes, upstreams(2), width // TILE, hidden_dim))

    def taylor_last():
        done = CHUNKS - 1
        dqs, (dk, dv) = taylor_back([done], (made[turns]["dk"], made[turns]["dv"]))
        dqs = [made[turns - done + 1 + m]["dq"] for m in range(done)] + dqs
        grad = jnp.concatenate([jnp.concatenate(dqs, axis=0), dk, dv], axis=1).astype(BF16)
        parts = folded(
            grad_in(turned_of(0), [([grad], 0, b_cols // tile)], b_cols, tile),
            grad_out(
                [made[m]["mix"] for m in range(CHUNKS)], upstreams(0), width // TILE, hidden_dim
            ),
        )
        return {"linear": grad, **parts}

    def taylor_final():
        came = jnp.concatenate(upstreams(0), axis=0)
        grad_inputs = rms_backward(
            feed.astype(F32), gain_row, nt(rest["linear"], pack_in[:, :taylor_cols])
        )
        return {"returned": (came.astype(F32) + grad_inputs).astype(BF16)}

    made.append(
        branches(
            {"a": a_shape, **taylor_shapes},
            [taylor_turn_back(CHUNKS - 2), dense_first(1), window_first, dense_first(3)],
        )
    )
    axes = ("dp", "seq")
    a, sent[-1]["out"] = lax.optimization_barrier((made[turns]["a"], sent[-1]["out"]))
    sum_a = lax.psum_scatter(a, axes, scatter_dimension=0, tiled=True)
    rest = branches(
        {"rest": rest_shape, "linear": ((length, taylor_cols), BF16)},
        [taylor_last, dense_second(1), window_second, dense_second(3)],
    )
    long = ((length, width), BF16)
    settled = branches(
        {"returned": long, "final": long}, [taylor_final, None, None, dense_final]
    )
    sum_a, rest["rest"] = lax.optimization_barrier((sum_a, rest["rest"]))
    sum_rest = lax.psum_scatter(rest["rest"], axes, scatter_dimension=0, tiled=True)[0]
    block_out = spread(swapped(settled["final"].reshape(2, block, width)), last)
    grad_tokens = spread(swapped(settled["returned"].reshape(2, block, width)), 0)

    place = lax.axis_index("dp") * lax.axis_size("seq") + seq
    gain_part = lax.dynamic_slice_in_dim(gain_row[0], place * fold, fold, 0)
    out_in, out_out, out_gain = result(
        jnp.stack([section, place]),
        sum_a,
        sum_rest,
        gain_part[:, None],
        pack_in,
        hidden_dim,
        padded,
        owners,
        window_cols,
        taylor_cols,
    )
    return (
        block_out,
        grad_tokens,
        out_in[None],
        out_out[None],
        out_gain[:, 0][None],
    )


def solution(mesh):
    placed = (
        P("dp", "seq", None),
        P("section", None, None),
        P("section", None, None),
        P("section", None),
        P("dp", None),
        P("dp", "seq", None),
    )
    return jax.shard_map(
        local,
        mesh=mesh,
        in_specs=placed,
        out_specs=(
            P("dp", "seq", "section"),
            P("dp", "seq", "section"),
            P("section", ("dp", "seq"), None),
            P("section", ("dp", "seq"), None),
            P("section", ("dp", "seq")),
        ),
        check_vma=False,
    )
```
